128 devices in a mesh: seq: 32 (over x_lo, z, y), mp: 4 (over x_hi, core).
Axes of the slice: x: 4 (x_hi: 2, x_lo: 2; x = x_hi * 2 + x_lo), y: 4, z: 4, core: 2. Of those that a mesh axis runs over, the one named last changes fastest.
Arguments:
- tokens: bfloat16 [16384, 1152], P('seq'), may hold values from -6 to 6
- grad_out: bfloat16 [16384, 1152], P('seq'), may hold values from -6 to 6
- attn_pre_gain: bfloat16 [1152], P('seq'), may hold values from 0.25 to 1.75
- w_query: bfloat16 [1152, 1024], P('seq', 'mp'), may hold values from -0.1875 to 0.1875
- query_gain: bfloat16 [256], P('seq'), may hold values from 0.25 to 1.75
- key_gain: bfloat16 [256], P('seq'), may hold values from 0.25 to 1.75
- w_keyval: bfloat16 [1152, 512], P(('seq', 'mp')), may hold values from -0.1875 to 0.1875
- w_out: bfloat16 [1024, 1152], P('mp', 'seq'), may hold values from -0.75 to 0.75
- attn_post_gain: bfloat16 [1152], P('seq'), may hold values from 0.25 to 1.75
- ffn_pre_gain: bfloat16 [1152], P('seq'), may hold values from 0.25 to 1.75
- w_gate: bfloat16 [1152, 6912], P('seq', 'mp'), may hold values from -0.1875 to 0.1875
- w_up: bfloat16 [1152, 6912], P('seq', 'mp'), may hold values from -0.1875 to 0.1875
- w_down: bfloat16 [6912, 1152], P('mp', 'seq'), may hold values from -0.078125 to 0.078125
- ffn_post_gain: bfloat16 [1152], P('seq'), may hold values from 0.25 to 1.75
Outputs:
- output: bfloat16 [16384, 1152], P('seq')
- grad_tokens: bfloat16 [16384, 1152], P('seq')
- grad_attn_pre_gain: float32 [1152], P('seq')
- grad_w_query: float32 [1152, 1024], P('seq', 'mp')
- grad_query_gain: float32 [256], P('seq')
- grad_key_gain: float32 [256], P('seq')
- grad_w_keyval: float32 [1152, 512], P(('seq', 'mp'))
- grad_w_out: float32 [1024, 1152], P('mp', 'seq')
- grad_attn_post_gain: float32 [1152], P('seq')
- grad_ffn_pre_gain: float32 [1152], P('seq')
- grad_w_gate: float32 [1152, 6912], P('seq', 'mp')
- grad_w_up: float32 [1152, 6912], P('seq', 'mp')
- grad_w_down: float32 [6912, 1152], P('mp', 'seq')
- grad_ffn_post_gain: float32 [1152], P('seq')
The draws below stay inside these ranges and needn't reach their ends.
All inputs are finite; a program needn't handle non-finite values.
Results may differ from the reference program's by a relative error of at most 0.03.
Values may be sent and summed in bfloat16 or wider, within the bound.
No kernel may reach another device: no remote copies, remote signals or barrier semaphores. Data moves between devices by JAX's collectives and lax.ppermute only.
A program may use at most 128 MiB of HBM per device.

```python
import jax
import jax.numpy as jnp
from jax import lax

D = 1152
H = 4
HD = 256
FF = 6912
WINDOW = 512
BLOCK = 512
LENGTH = 4096
SEQS = 4
TOKENS = 16384


def steps_of(rng, extent, pieces, low, high):
    level = 1.0
    for position, blocks in pieces:
        heights = jax.random.uniform(jax.random.fold_in(jax.random.fold_in(rng, 6), position), (blocks,), jnp.float32, low / len(pieces), high / len(pieces))
        level = level * jnp.repeat(jnp.exp(heights), extent[position] // blocks).reshape((-1,) + (1,) * (len(extent) - 1 - position))
    return level


def centred(stream_key, extent, width, bound, split=(), kind=jnp.bfloat16):
    level = steps_of(stream_key, extent, split, -0.22, 0.18) if split else 1.0
    entries = jax.random.normal(stream_key, extent, jnp.float32) * width * level
    return jnp.minimum(jnp.maximum(entries, -bound), bound).astype(kind)


def setup_inputs(seed: int = 0) -> dict:
    arg_keys = jax.random.split(jax.random.key(seed), 15)
    tokens = centred(arg_keys[0], (TOKENS, D), 1.0, 6.0, ((0, 32),))
    grad_out = centred(arg_keys[1], (TOKENS, D), 1.0, 6.0, ((0, 32),))
    attn_pre_gain = jnp.clip(1.0 + 0.15 * jax.random.normal(arg_keys[2], (D,), jnp.float32), 0.25, 1.75).astype(jnp.bfloat16)
    w_query = centred(arg_keys[3], (D, H * HD), D ** -0.5, 0.1875, ((0, 32), (1, 4)))
    query_gain = jnp.clip(1.0 + 0.15 * jax.random.normal(arg_keys[4], (HD,), jnp.float32), 0.25, 1.75).astype(jnp.bfloat16)
    key_gain = jnp.clip(1.0 + 0.15 * jax.random.normal(arg_keys[5], (HD,), jnp.float32), 0.25, 1.75).astype(jnp.bfloat16)
    w_keyval = centred(arg_keys[6], (D, 2 * HD), D ** -0.5, 0.1875, ((0, 128),))
    w_out = centred(arg_keys[7], (H * HD, D), (max(H * HD // 16, 1)) ** -0.5, 0.75, ((0, 4), (1, 32)))
    attn_post_gain = jnp.clip(1.0 + 0.15 * jax.random.normal(arg_keys[8], (D,), jnp.float32), 0.25, 1.75).astype(jnp.bfloat16)
    ffn_pre_gain = jnp.clip(1.0 + 0.15 * jax.random.normal(arg_keys[9], (D,), jnp.float32), 0.25, 1.75).astype(jnp.bfloat16)
    w_gate = centred(arg_keys[10], (D, FF), D ** -0.5, 0.1875, ((0, 32), (1, 4)))
    w_up = centred(arg_keys[11], (D, FF), D ** -0.5, 0.1875, ((0, 32), (1, 4)))
    w_down = centred(arg_keys[12], (FF, D), FF ** -0.5, 0.078125, ((0, 4), (1, 32)))
    ffn_post_gain = jnp.clip(1.0 + 0.15 * jax.random.normal(arg_keys[13], (D,), jnp.float32), 0.25, 1.75).astype(jnp.bfloat16)
    return dict(tokens=tokens, grad_out=grad_out, attn_pre_gain=attn_pre_gain, w_query=w_query, query_gain=query_gain, key_gain=key_gain, w_keyval=w_keyval, w_out=w_out, attn_post_gain=attn_post_gain, ffn_pre_gain=ffn_pre_gain, w_gate=w_gate, w_up=w_up, w_down=w_down, ffn_post_gain=ffn_post_gain)


EPS = 1e-06
SCALE = 0.0625
MASKED = -1e+30
HIGHEST_MODE = lax.Precision.HIGHEST

@jax.custom_vjp
def low(v):
    return lax.optimization_barrier(v.astype(jnp.bfloat16)).astype(jnp.float32)

@jax.custom_vjp
def low_back(v):
    return v

def low_keep(v):
    return (low(v), None)

def low_pass(kept, grad):
    return (grad,)

def back_keep(v):
    return (v, None)

def back_low(kept, grad):
    return (low(grad),)
low.defvjp(low_keep, low_pass)
low_back.defvjp(back_keep, back_low)

def rms_norm(values, gain):
    return values * lax.rsqrt(lax.optimization_barrier(jnp.mean(values * values, axis=-1, keepdims=True)) + EPS) * gain

def rotary(values, angle):
    half_width = values.shape[-1] // 2
    former = values[..., :half_width]
    latter = values[..., half_width:]
    cosine = jnp.cos(angle)
    sine = jnp.sin(angle)
    return jnp.concatenate([former * cosine - latter * sine, latter * cosine + former * sine], axis=-1)

def gelu_tanh(values):
    return 0.5 * values * (1.0 + jnp.tanh(0.7978845608028654 * (values + 0.044715 * values * values * values)))

def angles(row_start, count):
    positions = (row_start + jnp.arange(count, dtype=jnp.int32)).astype(jnp.float32)
    exponent = jnp.arange(HD // 2, dtype=jnp.float32) * (-2.0 / HD)
    return positions[:, None] * jnp.power(10000.0, exponent)[None, :]

def allowed_mask(row_count, first_pos):
    row_ids = jnp.arange(row_count, dtype=jnp.int32)[:, None]
    key_ids = jnp.arange(row_count + WINDOW, dtype=jnp.int32)[None, :]
    return (key_ids > row_ids) & (key_ids <= row_ids + WINDOW) & (key_ids + first_pos >= WINDOW)

def attend(query, keys, values):
    row_count = min(BLOCK, 512)
    padded_keys = jnp.concatenate([jnp.zeros((WINDOW, HD), keys.dtype), keys], axis=0)
    padded_values = jnp.concatenate([jnp.zeros((WINDOW, HD), values.dtype), values], axis=0)

    def one_block(block_index):
        row_start = (block_index * row_count).astype(jnp.int32)
        query_part = lax.dynamic_slice_in_dim(query, row_start, row_count, 0)
        key_part = lax.dynamic_slice_in_dim(padded_keys, row_start, row_count + WINDOW, 0)
        value_part = lax.dynamic_slice_in_dim(padded_values, row_start, row_count + WINDOW, 0)
        score = low_back(jnp.einsum('rhd,kd->hrk', query_part, key_part, precision=HIGHEST_MODE) * SCALE)
        score = jnp.where(allowed_mask(row_count, row_start)[None], score, MASKED)
        peak = lax.optimization_barrier(jnp.max(score, axis=-1, keepdims=True))
        weight = jnp.exp(score - peak)
        prob = weight / lax.optimization_barrier(jnp.sum(weight, axis=-1, keepdims=True))
        return jnp.einsum('hrk,kd->rhd', low(prob), value_part, precision=HIGHEST_MODE)
    parts = lax.map(jax.checkpoint(one_block), jnp.arange(LENGTH // row_count, dtype=jnp.int32))
    return parts.reshape(LENGTH, H, HD)

def block_layer(inputs, attn_pre_gain, w_query, query_gain, key_gain, w_keyval, w_out, attn_post_gain, ffn_pre_gain, w_gate, w_up, w_down, ffn_post_gain):
    normed_x = low(rms_norm(inputs, attn_pre_gain))
    query_raw = low_back(jnp.dot(normed_x, w_query, precision=HIGHEST_MODE)).reshape(LENGTH, H, HD)
    keyval_raw = low_back(jnp.dot(normed_x, w_keyval, precision=HIGHEST_MODE))
    angle = angles(0, LENGTH)
    query = low(rotary(rms_norm(query_raw, query_gain), angle[:, None, :]))
    keys = low(rotary(rms_norm(keyval_raw[:, :HD], key_gain), angle))
    values = low(keyval_raw[:, HD:])
    attended = low_back(low(attend(query, keys, values))).reshape(LENGTH, H * HD)
    branch = low_back(jnp.dot(attended, w_out, precision=HIGHEST_MODE))
    middle = inputs + rms_norm(branch, attn_post_gain)
    normed_mid = low(rms_norm(middle, ffn_pre_gain))
    gate = low_back(jnp.dot(normed_mid, w_gate, precision=HIGHEST_MODE))
    up_proj = low_back(jnp.dot(normed_mid, w_up, precision=HIGHEST_MODE))
    hidden = low(gelu_tanh(gate) * up_proj)
    ffn_out = low_back(jnp.dot(hidden, w_down, precision=HIGHEST_MODE))
    return middle + rms_norm(ffn_out, ffn_post_gain)

def reference(tokens, grad_out, attn_pre_gain, w_query, query_gain, key_gain, w_keyval, w_out, attn_post_gain, ffn_pre_gain, w_gate, w_up, w_down, ffn_post_gain):
    params = tuple((item.astype(jnp.float32) for item in (attn_pre_gain, w_query, query_gain, key_gain, w_keyval, w_out, attn_post_gain, ffn_pre_gain, w_gate, w_up, w_down, ffn_post_gain)))
    inputs_all = tokens.astype(jnp.float32).reshape(SEQS, LENGTH, D)
    cot_all = grad_out.astype(jnp.float32).reshape(SEQS, LENGTH, D)
    zero_grads = tuple((jnp.zeros(item.shape, jnp.float32) for item in params))

    def per_sequence(totals, pair):
        inputs, cotangent = pair
        result, pull = jax.vjp(block_layer, inputs, *params)
        grads = pull(cotangent)
        totals = tuple((acc + item for acc, item in zip(totals, grads[1:])))
        return (totals, (result.astype(jnp.bfloat16), grads[0].astype(jnp.bfloat16)))
    totals, (results, input_grads) = lax.scan(per_sequence, zero_grads, (inputs_all, cot_all))
    return (results.reshape(TOKENS, D), input_grads.reshape(TOKENS, D), totals[0], totals[1], totals[2], totals[3], totals[4], totals[5], totals[6], totals[7], totals[8], totals[9], totals[10], totals[11])
```

```python
import jax
import jax.numpy as jnp
from jax import lax
from jax.sharding import PartitionSpec as P

D = 1152
HD = 256
WINDOW = 512
SEQ_BLOCKS = 8
ROWS = 128
KEYS = ROWS + WINDOW
EPS = 1e-06
SCALE = 0.0625
MASKED = -1e30
SIZES = {"xl": 2, "z": 4, "y": 4, "xh": 2, "c": 2}
CUT = 896

bf16 = jnp.bfloat16
f32 = jnp.float32


def coords(n):
    mp, s = n % 4, n // 4
    return {"xl": s // 16, "z": s // 4 % 4, "y": s % 4, "xh": mp // 2, "c": mp % 2}


def flat(at):
    return ((at["xl"] * 4 + at["z"]) * 4 + at["y"]) * 4 + at["xh"] * 2 + at["c"]


def fetch(x, **delta):
    pairs = []
    for n in range(128):
        at = coords(n)
        for axis, by in delta.items():
            at[axis] = (at[axis] + by) % SIZES[axis]
        pairs.append((flat(at), n))
    return lax.ppermute(x, ("seq", "mp"), pairs)


def fetch_line(x, by):
    pairs = [(n + by, n) for n in range(128) if 0 <= n + by < 128]
    return lax.ppermute(x, ("seq", "mp"), pairs)


def gather_small(x, axis):
    return [x] + [fetch(x, **{axis: k}) for k in (1, 2, 3)]


def gather_big(x, axis):
    one = fetch(x, **{axis: 1})
    three = fetch(x, **{axis: 3})
    two = [fetch(one[:2], **{axis: 1}), fetch(three[2:], **{axis: 3})]
    return [x, one, jnp.concatenate(two, axis=0), three]


def gather_grid(x, route, big):
    first, second = ("z", "y") if route == 0 else ("y", "z")
    line = jnp.stack(gather_small(x, first))
    parts = (gather_big if big else gather_small)(line, second)
    return jnp.stack(parts, axis=1 if route == 0 else 0).reshape(D, x.shape[-1])


def add(*terms):
    total = terms[0].astype(f32)
    for term in terms[1:]:
        total = total + term.astype(f32)
    return total


def scatter_small(blocks, axis):
    return add(blocks[0], *[fetch(blocks[k], **{axis: 4 - k}) for k in (1, 2, 3)])


def scatter_big(blocks, axis):
    up = fetch(blocks[2][:2], **{axis: 3})
    down = fetch(blocks[2][2:], **{axis: 1})
    one = jnp.concatenate([add(blocks[1][:2], up).astype(bf16), blocks[1][2:]], axis=0)
    three = jnp.concatenate([blocks[3][:2], add(blocks[3][2:], down).astype(bf16)], axis=0)
    return add(blocks[0], fetch(one, **{axis: 3}), fetch(three, **{axis: 1}))


def scatter_grid(x, route, big):
    first, second = ("z", "y") if route == 0 else ("y", "z")
    grid = x.reshape(4, 4, 72, x.shape[-1])
    blocks = [grid[:, k] if route == 0 else grid[k] for k in range(4)]
    line = (scatter_big if big else scatter_small)(blocks, second).astype(bf16)
    return scatter_small([line[k] for k in range(4)], first)


def gather_rows(x):
    core = fetch(x, c=1)
    far = fetch(x, xh=1)
    return jnp.concatenate([x, core, far, fetch(far, c=1)], axis=0)


def scatter_rows(x):
    got = [fetch(x[ROWS : 2 * ROWS], c=1), fetch(x[3 * ROWS :], c=1)]
    far = add(x[2 * ROWS : 3 * ROWS], got[1]).astype(bf16)
    return add(x[:ROWS], got[0], fetch(far, xh=1))


def in_order(rows, xh, c):
    grid = rows.reshape(2, 2, ROWS, rows.shape[-1])
    grid = jnp.where(xh == 0, grid, grid[::-1])
    return jnp.where(c == 0, grid, grid[:, ::-1]).reshape(rows.shape)


def dot(a, b):
    return jnp.dot(a, b, preferred_element_type=f32)


def dot_nt(a, b):
    return lax.dot_general(a, b, (((1,), (1,)), ((), ())), preferred_element_type=f32)


def dot_tn(a, b):
    return lax.dot_general(a, b, (((0,), (0,)), ((), ())), preferred_element_type=f32)


def inverse_rms(v):
    return lax.rsqrt(jnp.mean(v * v, axis=-1, keepdims=True) + EPS)


def norm_back(v, r, g, e):
    ev = e * v
    inner = jnp.mean(g * ev, axis=-1, keepdims=True)
    gain_axes = tuple(range(v.ndim - 1))
    return r * (g * e) - v * (r * r * r * inner), jnp.sum(ev * r, axis=gain_axes)


def rotary(v, cosine, sine):
    former, latter = v[..., :128], v[..., 128:]
    return jnp.concatenate([former * cosine - latter * sine, latter * cosine + former * sine], axis=-1)


def gelu_tanh(v):
    return 0.5 * v * (1.0 + jnp.tanh(0.7978845608028654 * (v + 0.044715 * v * v * v)))


def gated_hidden(gate_in, up_in):
    return gelu_tanh(gate_in) * up_in


def per_device(
    tokens,
    grad_out,
    attn_pre_gain,
    w_query,
    query_gain,
    key_gain,
    w_keyval,
    w_out,
    attn_post_gain,
    ffn_pre_gain,
    w_gate,
    w_up,
    w_down,
    ffn_post_gain,
):
    seq = lax.axis_index("seq")
    mp = lax.axis_index("mp")
    xl, z, y = seq // 16, seq // 4 % 4, seq % 4
    xh, c = mp // 2, mp % 2

    kv_mine = lax.dynamic_slice_in_dim(w_keyval, 256 * c, 256, 1)
    kv_other = fetch(lax.dynamic_slice_in_dim(w_keyval, 256 * (1 - c), 256, 1), c=1)
    kv18 = jnp.where(
        c == 0,
        jnp.concatenate([kv_mine, kv_other], axis=0),
        jnp.concatenate([kv_other, kv_mine], axis=0),
    )
    short = jnp.pad(jnp.stack([query_gain, key_gain], axis=1), ((0, 28), (0, 0)))
    gains = jnp.stack([attn_pre_gain, attn_post_gain, ffn_pre_gain, ffn_post_gain], axis=1)
    gains = jnp.pad(jnp.concatenate([gains, short], axis=1), ((0, 0), (0, 122)))
    parcel = jnp.concatenate([w_query, gains, w_out.T, kv18.reshape(36, 128)], axis=1)
    parcels = [
        [parcel, fetch(parcel, xh=1)],
        [fetch(parcel, xl=1), fetch(parcel, xl=1, xh=1)],
    ]

    def kv36(pair):
        own, far = pair[0][:, 640:].reshape(18, 256), pair[1][:, 640:].reshape(18, 256)
        return jnp.where(
            xh == 0, jnp.concatenate([own, far], axis=0), jnp.concatenate([far, own], axis=0)
        )

    block_a = jnp.concatenate(
        [jnp.concatenate([p[0][:, :256], p[1][:, :256], p[0][:, 256:384]], axis=1) for p in parcels],
        axis=0,
    )
    block_b = jnp.concatenate(
        [jnp.concatenate([kv36(p), p[0][:, 384:640], p[1][:, 384:640]], axis=1) for p in parcels],
        axis=0,
    )
    part_a = gather_grid(block_a, 0, False)
    part_b = gather_grid(block_b, 1, False)
    part_ao = fetch(part_a[:, :512], c=1)
    part_bo = fetch(part_b, c=1)

    ffn_own = jnp.stack([w_gate, w_up, w_down.T])
    ffn_pair = jnp.concatenate([ffn_own, fetch(ffn_own, xl=1)], axis=1)
    gate_weight = gather_grid(ffn_pair[0], 0, True)
    up_weight = gather_grid(ffn_pair[1], 1, True)
    down_a = gather_grid(ffn_pair[2][:, :CUT], 0, True)
    down_b = gather_grid(ffn_pair[2][:, CUT:], 1, True)

    half = fetch_line(lax.dynamic_slice_in_dim(tokens, 256 * c, 256, 0), -4)
    half_other = fetch(half, c=1)
    before = jnp.where(
        c == 0,
        jnp.concatenate([half, half_other], axis=0),
        jnp.concatenate([half_other, half], axis=0),
    )
    rows = lax.dynamic_slice_in_dim(jnp.concatenate([before, tokens], axis=0), ROWS * mp, KEYS, 0)
    column = jnp.arange(D, dtype=jnp.int32)
    zr, yr, xr, place = column // 288, column // 72 % 4, column // 36 % 2, column % 36
    owner = (xl ^ xr) * 16 + (z + zr) % 4 * 4 + (y + yr) % 4
    order = (column[:, None] == (owner * 36 + place)[None, :]).astype(bf16)
    short_owner = jnp.where(place < 8, owner * 8 + place, -1)
    short_order = (short_owner[:, None] == jnp.arange(HD, dtype=jnp.int32)[None, :]).astype(bf16)
    x_keys = dot(rows, order).astype(bf16).astype(f32)
    x = x_keys[WINDOW:]
    e_out = dot(lax.dynamic_slice_in_dim(grad_out, ROWS * mp, ROWS, 0), order).astype(bf16).astype(f32)
    r_keys = inverse_rms(x_keys)

    gain_cols = part_a[:, 512:]
    gain_rows = gain_cols[:, :8].T.astype(f32)
    pre_gain, post_gain, ffn_pre, ffn_post = (gain_rows[k : k + 1] for k in range(4))
    short_rows = dot_tn(gain_cols, short_order)
    qnorm_gain, knorm_gain = short_rows[4:5], short_rows[5:6]

    first_pos = seq % SEQ_BLOCKS * 512 + ROWS * mp
    positions = (first_pos - WINDOW + jnp.arange(KEYS, dtype=jnp.int32)).astype(f32)
    exponent = jnp.arange(HD // 2, dtype=f32) * (-2.0 / HD)
    angle = positions[:, None] * jnp.power(10000.0, exponent)[None, :]
    cosine, sine = jnp.cos(angle), jnp.sin(angle)
    cos_q, sin_q = cosine[WINDOW:], sine[WINDOW:]
    xn_keys = (x_keys * r_keys * pre_gain).astype(bf16)
    xn = xn_keys[WINDOW:]
    q_raw = [dot(xn, part_a[:, :512]), dot(xn, part_ao)]
    q_raw = jnp.stack([q_raw[h // 2][:, h % 2 * HD : h % 2 * HD + HD] for h in range(4)])
    kv_here, kv_there = dot(xn_keys, part_b[:, :HD]), dot(xn_keys, part_bo[:, :HD])
    key_raw = jnp.where(c == 0, kv_here, kv_there)
    values = jnp.where(c == 0, kv_there, kv_here).astype(bf16)
    r_q, r_k = inverse_rms(q_raw), inverse_rms(key_raw)
    query = rotary(q_raw * r_q * qnorm_gain, cos_q, sin_q).astype(bf16).reshape(4 * ROWS, HD)
    keys = rotary(key_raw * r_k * knorm_gain, cosine, sine).astype(bf16)
    row_ids = jnp.arange(ROWS, dtype=jnp.int32)[:, None]
    key_ids = jnp.arange(KEYS, dtype=jnp.int32)[None, :]
    allowed = (key_ids > row_ids) & (key_ids <= row_ids + WINDOW) & (key_ids + first_pos >= WINDOW)
    score = dot_nt(query, keys).reshape(4, ROWS, KEYS) * SCALE
    score = jnp.where(allowed[None], score, MASKED)
    peak = jnp.max(score, axis=-1, keepdims=True)
    weight = jnp.exp(score - peak)
    prob = weight / jnp.sum(weight, axis=-1, keepdims=True)
    prob_low = prob.astype(bf16).reshape(4 * ROWS, KEYS)
    att = dot(prob_low, values).astype(bf16).reshape(4, ROWS, HD)
    att = jnp.concatenate([att[h] for h in range(4)], axis=1)
    out_own, out_other = part_b[:, HD:], part_bo[:, HD:]
    branch = dot_nt(att[:, :512], out_own) + dot_nt(att[:, 512:], out_other)
    r_branch = inverse_rms(branch)
    mid = x + branch * r_branch * post_gain
    r_mid = inverse_rms(mid)
    hn_rows = (mid * r_mid * ffn_pre).astype(bf16)

    hn = gather_rows(hn_rows)
    gate = dot(hn, gate_weight)
    up = dot(hn, up_weight)
    hidden = gated_hidden(gate, up).astype(bf16)
    hidden_a, hidden_b = hidden[:, :CUT], hidden[:, CUT:]
    ffn = scatter_rows((dot_nt(hidden_a, down_a) + dot_nt(hidden_b, down_b)).astype(bf16))
    r_ffn = inverse_rms(ffn)
    output_rows = (mid + ffn * r_ffn * ffn_post).astype(bf16)
    d_ffn_rows, grad_ffn_post = norm_back(ffn, r_ffn, ffn_post, e_out)
    d_ffn = gather_rows(d_ffn_rows.astype(bf16))
    d_hidden = jnp.concatenate([dot(d_ffn, down_a), dot(d_ffn, down_b)], axis=1)
    _, gate_pull = jax.vjp(gated_hidden, gate, up)
    d_gate, d_up = gate_pull(d_hidden)
    d_gate, d_up = d_gate.astype(bf16), d_up.astype(bf16)
    d_hn = scatter_rows((dot_nt(d_gate, gate_weight) + dot_nt(d_up, up_weight)).astype(bf16))
    g_down_a = scatter_grid(dot_tn(d_ffn, hidden_a).astype(bf16), 0, True)
    g_down_b = scatter_grid(dot_tn(d_ffn, hidden_b).astype(bf16), 1, True)
    g_gate = scatter_grid(dot_tn(hn, d_gate).astype(bf16), 0, True)
    g_up = scatter_grid(dot_tn(hn, d_up).astype(bf16), 1, True)
    g_ffn = jnp.stack([g_gate, g_up, jnp.concatenate([g_down_a, g_down_b], axis=1)])
    g_ffn = add(g_ffn[:, :36], fetch(g_ffn[:, 36:].astype(bf16), xl=1))

    d_mid, grad_ffn_pre = norm_back(mid, r_mid, ffn_pre, d_hn)
    d_mid = d_mid + e_out
    d_branch, grad_post = norm_back(branch, r_branch, post_gain, d_mid)
    d_branch = d_branch.astype(bf16)
    d_att = [dot(d_branch, out_own), dot(d_branch, out_other)]
    d_att = jnp.stack([d_att[h // 2][:, h % 2 * HD : h % 2 * HD + HD] for h in range(4)])
    d_att = d_att.astype(bf16).reshape(4 * ROWS, HD)
    d_prob = dot_nt(d_att, values).reshape(4, ROWS, KEYS)
    delta = jnp.sum(prob * d_prob, axis=-1, keepdims=True)
    d_score = (prob * (d_prob - delta)).astype(bf16).reshape(4 * ROWS, KEYS)
    d_query = dot(d_score, keys).reshape(4, ROWS, HD) * SCALE
    d_kv = jnp.concatenate(
        [dot_tn(d_score, query) * SCALE, dot_tn(prob_low, d_att)], axis=1
    ).reshape(5, ROWS, 2 * HD)
    d_kv_low = d_kv[:4].astype(bf16)
    d_kv = add(d_kv[4], *[fetch_line(d_kv_low[k], 4 - k) for k in range(4)])
    d_key = rotary(d_kv[:, :HD], cos_q, -sin_q)
    d_key_raw, grad_key_gain = norm_back(key_raw[WINDOW:], r_k[WINDOW:], knorm_gain, d_key)
    d_key_raw = d_key_raw.astype(bf16)
    d_value = d_kv[:, HD:].astype(bf16)
    d_here = jnp.where(c == 0, d_key_raw, d_value)
    d_there = jnp.where(c == 0, d_value, d_key_raw)
    d_q_raw, grad_query_gain = norm_back(q_raw, r_q, qnorm_gain, rotary(d_query, cos_q, -sin_q))
    d_q_raw = d_q_raw.astype(bf16)
    d_q_own = jnp.concatenate([d_q_raw[0], d_q_raw[1]], axis=1)
    d_q_other = jnp.concatenate([d_q_raw[2], d_q_raw[3]], axis=1)
    d_xn = (
        dot_nt(d_q_own, part_a[:, :512])
        + dot_nt(d_q_other, part_ao)
        + dot_nt(d_here, part_b[:, :HD])
        + dot_nt(d_there, part_bo[:, :HD])
    )
    d_x, grad_pre = norm_back(x, r_keys[WINDOW:], pre_gain, d_xn)
    d_tokens = (d_mid + d_x).astype(bf16)

    def finished(values_low):
        return in_order(gather_rows(dot_nt(values_low, order).astype(bf16)), xh, c)

    output = finished(output_rows)
    grad_tokens = finished(d_tokens)

    short_grads = dot_nt(jnp.stack([grad_query_gain, grad_key_gain]).astype(bf16), short_order)
    gain_grads = jnp.concatenate(
        [jnp.stack([grad_pre, grad_post, grad_ffn_pre, grad_ffn_post]), short_grads]
    )
    gain_grads = jnp.pad(gain_grads, ((0, 2), (0, 0))).T.astype(bf16)
    gain_grads = jnp.pad(gain_grads, ((0, 0), (0, 120)))
    own_a = jnp.concatenate([dot_tn(xn, d_q_own).astype(bf16), gain_grads], axis=1)
    other_a = jnp.concatenate([dot_tn(xn, d_q_other).astype(bf16), gain_grads], axis=1)
    own_b = jnp.concatenate([dot_tn(xn, d_here), dot_tn(d_branch, att[:, :512])], axis=1)
    other_b = jnp.concatenate([dot_tn(xn, d_there), dot_tn(d_branch, att[:, 512:])], axis=1)
    sum_a = add(own_a, fetch(other_a, c=1)).astype(bf16)
    sum_b = add(own_b, fetch(other_b.astype(bf16), c=1)).astype(bf16)
    sum_a = scatter_grid(sum_a, 0, False).astype(bf16)
    sum_b = scatter_grid(sum_b, 1, False).astype(bf16)

    def parcel_back(xr_, xhr):
        a, b = sum_a[36 * xr_ : 36 * xr_ + 36], sum_b[36 * xr_ : 36 * xr_ + 36]
        kv = jnp.where(xh ^ xhr == 0, b[:18, :HD], b[18:, :HD]).reshape(36, 128)
        return jnp.concatenate(
            [a[:, 256 * xhr : 256 * xhr + 256], a[:, 512:], b[:, 256 + 256 * xhr : 512 + 256 * xhr], kv],
            axis=1,
        )

    total = add(
        parcel_back(0, 0),
        fetch(parcel_back(0, 1), xh=1),
        fetch(parcel_back(1, 0), xl=1),
        fetch(parcel_back(1, 1), xl=1, xh=1),
    )
    g_kv = total[:, 640:].reshape(18, 256)
    g_kv_here = jnp.where(c == 0, g_kv[:9], g_kv[9:])
    g_kv_away = fetch(jnp.where(c == 0, g_kv[9:], g_kv[:9]).astype(bf16), c=1).astype(f32)
    g_keyval = jnp.where(
        c == 0,
        jnp.concatenate([g_kv_here, g_kv_away], axis=1),
        jnp.concatenate([g_kv_away, g_kv_here], axis=1),
    )
    g_gains = total[:, 256:264].T
    return (
        output,
        grad_tokens,
        g_gains[0],
        total[:, :256],
        g_gains[4, :8],
        g_gains[5, :8],
        g_keyval,
        total[:, 384:640].T,
        g_gains[1],
        g_gains[2],
        g_ffn[0],
        g_ffn[1],
        g_ffn[2].T,
        g_gains[3],
    )


def solution(mesh):
    row, vector, weight, weight_t = P("seq", None), P("seq"), P("seq", "mp"), P("mp", "seq")
    keyval = P(("seq", "mp"), None)
    return jax.shard_map(
        per_device,
        mesh=mesh,
        in_specs=(row, row, vector, weight, vector, vector, keyval, weight_t)
        + (vector, vector, weight, weight, weight_t, vector),
        out_specs=(row, row, vector, weight, vector, vector, keyval, weight_t)
        + (vector, vector, weight, weight, weight_t, vector),
        check_vma=False,
    )
```

```python
import jax
import jax.numpy as jnp
from jax import lax
from jax.experimental import pallas as pl
from jax.experimental.pallas import tpu as pltpu
from jax.sharding import PartitionSpec as P

D = 1152
HD = 256
WINDOW = 512
SEQ_BLOCKS = 8
ROWS = 128
KEYS = ROWS + WINDOW
EPS = 1e-06
SCALE = 0.0625
MASKED = -1e30
SIZES = {"xl": 2, "z": 4, "y": 4, "xh": 2, "c": 2}
CUT = 896

bf16 = jnp.bfloat16
f32 = jnp.float32


def coords(n):
    mp, s = n % 4, n // 4
    return {"xl": s // 16, "z": s // 4 % 4, "y": s % 4, "xh": mp // 2, "c": mp % 2}


def flat(at):
    return ((at["xl"] * 4 + at["z"]) * 4 + at["y"]) * 4 + at["xh"] * 2 + at["c"]


def fetch(x, **delta):
    pairs = []
    for n in range(128):
        at = coords(n)
        for axis, by in delta.items():
            at[axis] = (at[axis] + by) % SIZES[axis]
        pairs.append((flat(at), n))
    return lax.ppermute(x, ("seq", "mp"), pairs)


def fetch_line(x, by):
    pairs = [(n + by, n) for n in range(128) if 0 <= n + by < 128]
    return lax.ppermute(x, ("seq", "mp"), pairs)


def gather_small(x, axis):
    return [x] + [fetch(x, **{axis: k}) for k in (1, 2, 3)]


def gather_big(x, axis):
    one = fetch(x, **{axis: 1})
    three = fetch(x, **{axis: 3})
    two = [fetch(one[:2], **{axis: 1}), fetch(three[2:], **{axis: 3})]
    return [x, one, jnp.concatenate(two, axis=0), three]


def gather_grids(a, b):
    line_a, line_b = gather_small(a, "z"), gather_small(b, "y")
    line_a, line_b = lax.optimization_barrier((line_a, line_b))
    grid_a = jnp.stack(gather_big(jnp.stack(line_a), "y"), axis=1)
    grid_b = jnp.stack(gather_big(jnp.stack(line_b), "z"), axis=0)
    return grid_a.reshape(D, a.shape[-1]), grid_b.reshape(D, b.shape[-1])


def add(*terms):
    total = terms[0].astype(f32)
    for term in terms[1:]:
        total = total + term.astype(f32)
    return total


def scatter_small(blocks, axis):
    return add(blocks[0], *[fetch(blocks[k], **{axis: 4 - k}) for k in (1, 2, 3)])


def blocks_of(parts, route):
    grids = [part.reshape(4, 4, 72, part.shape[-1]) for part in parts]
    return [
        jnp.concatenate([grid[:, k] if route == 0 else grid[k] for grid in grids], axis=-1)
        for k in range(4)
    ]


def halves_out(blocks, axis):
    return fetch(blocks[2][:2], **{axis: 3}), fetch(blocks[2][2:], **{axis: 1})


def sides_out(blocks, halves, axis):
    one = jnp.concatenate([add(blocks[1][:2], halves[0]).astype(bf16), blocks[1][2:]], axis=0)
    three = jnp.concatenate([blocks[3][:2], add(blocks[3][2:], halves[1]).astype(bf16)], axis=0)
    return fetch(one, **{axis: 3}), fetch(three, **{axis: 1})


def gather_rows(x):
    core = fetch(x, c=1)
    far = fetch(x, xh=1)
    return jnp.concatenate([x, core, far, fetch(far, c=1)], axis=0)


def scatter_rows(x):
    got = [fetch(x[ROWS : 2 * ROWS], c=1), fetch(x[3 * ROWS :], c=1)]
    far = add(x[2 * ROWS : 3 * ROWS], got[1]).astype(bf16)
    return add(x[:ROWS], got[0], fetch(far, xh=1))


def in_order(rows, xh, c):
    grid = rows.reshape(2, 2, ROWS, rows.shape[-1])
    grid = jnp.where(xh == 0, grid, grid[::-1])
    return jnp.where(c == 0, grid, grid[:, ::-1]).reshape(rows.shape)


def dot(a, b):
    return jnp.dot(a, b, preferred_element_type=f32)


def dot_nt(a, b):
    return lax.dot_general(a, b, (((1,), (1,)), ((), ())), preferred_element_type=f32)


def dot_tn(a, b):
    return lax.dot_general(a, b, (((0,), (0,)), ((), ())), preferred_element_type=f32)


def inverse_rms(v):
    return lax.rsqrt(jnp.mean(v * v, axis=-1, keepdims=True) + EPS)


def norm_back(v, r, g, e):
    ev = e * v
    inner = jnp.mean(g * ev, axis=-1, keepdims=True)
    gain_axes = tuple(range(v.ndim - 1))
    return r * (g * e) - v * (r * r * r * inner), jnp.sum(ev * r, axis=gain_axes)


def rotary(v, cosine, sine):
    former, latter = v[..., :128], v[..., 128:]
    return jnp.concatenate([former * cosine - latter * sine, latter * cosine + former * sine], axis=-1)


def gelu_tanh(v):
    return 0.5 * v * (1.0 + jnp.tanh(0.7978845608028654 * (v + 0.044715 * v * v * v)))


def gated_hidden(gate_in, up_in):
    return gelu_tanh(gate_in) * up_in


def in_vmem(count):
    return [pl.BlockSpec(memory_space=pltpu.VMEM)] * count


def forward_kernel(hn_ref, w_ref, prior_ref, gate_ref, up_ref, sum_ref):
    hn = hn_ref[...]
    gate = dot(hn, w_ref[:, :CUT])
    up = dot(hn, w_ref[:, CUT : 2 * CUT])
    hidden = gated_hidden(gate, up).astype(bf16)
    gate_ref[...] = gate.astype(bf16)
    up_ref[...] = up.astype(bf16)
    total = dot_nt(hidden, w_ref[:, 2 * CUT :])
    if prior_ref is not None:
        total = total + prior_ref[...]
    sum_ref[...] = total.astype(sum_ref.dtype)


def ffn_forward(hn, w, prior):
    first = prior is None
    rows = hn.shape[0]
    kernel = (lambda a, b, *out: forward_kernel(a, b, None, *out)) if first else forward_kernel
    args = (hn, w) if first else (hn, w, prior)
    return pl.pallas_call(
        kernel,
        out_shape=(
            jax.ShapeDtypeStruct((rows, CUT), bf16),
            jax.ShapeDtypeStruct((rows, CUT), bf16),
            jax.ShapeDtypeStruct((rows, D), f32 if first else bf16),
        ),
        in_specs=in_vmem(len(args)),
        out_specs=tuple(in_vmem(3)),
        compiler_params=pltpu.CompilerParams(vmem_limit_bytes=36 * 2**20),
        cost_estimate=pl.CostEstimate(
            flops=6 * rows * D * CUT, bytes_accessed=12 * 2**20, transcendentals=rows * CUT
        ),
    )(*args)


def backward_kernel(d_ffn_ref, w_ref, gate_ref, up_ref, prior_ref, grads_ref, sum_ref):
    d_hidden = dot(d_ffn_ref[...], w_ref[:, 2 * CUT :])
    gate, up = gate_ref[...].astype(f32), up_ref[...].astype(f32)
    square = gate * gate
    tanh = jnp.tanh(0.7978845608028654 * (gate + 0.044715 * square * gate))
    half = 0.5 * (1.0 + tanh)
    gelu = gate * half
    slope = half + 0.5 * gate * (1.0 - tanh * tanh) * (
        0.7978845608028654 * (1.0 + 3 * 0.044715 * square)
    )
    d_gate = (d_hidden * up * slope).astype(bf16)
    d_up = (d_hidden * gelu).astype(bf16)
    grads_ref[0] = d_gate
    grads_ref[1] = d_up
    grads_ref[2] = (gelu * up).astype(bf16)
    total = dot_nt(d_gate, w_ref[:, :CUT]) + dot_nt(d_up, w_ref[:, CUT : 2 * CUT])
    if prior_ref is not None:
        total = total + prior_ref[...]
    sum_ref[...] = total.astype(sum_ref.dtype)


def ffn_backward(d_ffn, w, gate, up, prior):
    first = prior is None
    rows = d_ffn.shape[0]
    kernel = (
        (lambda a, b, g, u, *out: backward_kernel(a, b, g, u, None, *out)) if first else backward_kernel
    )
    args = (d_ffn, w, gate, up) if first else (d_ffn, w, gate, up, prior)
    return pl.pallas_call(
        kernel,
        out_shape=(
            jax.ShapeDtypeStruct((3, rows, CUT), bf16),
            jax.ShapeDtypeStruct((rows, D), f32 if first else bf16),
        ),
        in_specs=in_vmem(len(args)),
        out_specs=tuple(in_vmem(2)),
        compiler_params=pltpu.CompilerParams(vmem_limit_bytes=36 * 2**20),
        cost_estimate=pl.CostEstimate(
            flops=6 * rows * D * CUT, bytes_accessed=14 * 2**20, transcendentals=rows * CUT
        ),
    )(*args)


def weights_kernel(route, hn_ref, d_ffn_ref, grads_ref, out_ref):
    def product(left_ref):
        total = dot_tn(left_ref[...], grads_ref[0]).astype(bf16)
        for zr in range(4):
            for yr in range(4):
                block = total[72 * (4 * zr + yr) : 72 * (4 * zr + yr) + 72]
                if route == 0:
                    out_ref[yr, zr] = block
                else:
                    out_ref[zr, yr] = block

    which = pl.program_id(0)

    @pl.when(which < 2)
    def _():
        product(hn_ref)

    @pl.when(which == 2)
    def _():
        product(d_ffn_ref)


def ffn_weights(hn, d_ffn, grads, route):
    rows = hn.shape[0]
    whole = pl.BlockSpec((rows, D), lambda j: (0, 0))
    return pl.pallas_call(
        lambda *refs: weights_kernel(route, *refs),
        grid=(3,),
        out_shape=jax.ShapeDtypeStruct((4, 4, 72, 3 * CUT), bf16),
        in_specs=[whole, whole, pl.BlockSpec((1, rows, CUT), lambda j: (j, 0, 0))],
        out_specs=pl.BlockSpec((4, 4, 72, CUT), lambda j: (0, 0, 0, j)),
        compiler_params=pltpu.CompilerParams(vmem_limit_bytes=36 * 2**20),
        cost_estimate=pl.CostEstimate(
            flops=6 * rows * D * CUT, bytes_accessed=12 * 2**20, transcendentals=0
        ),
    )(hn, d_ffn, grads)


def per_device(
    tokens,
    grad_out,
    attn_pre_gain,
    w_query,
    query_gain,
    key_gain,
    w_keyval,
    w_out,
    attn_post_gain,
    ffn_pre_gain,
    w_gate,
    w_up,
    w_down,
    ffn_post_gain,
):
    seq = lax.axis_index("seq")
    mp = lax.axis_index("mp")
    xl, z, y = seq // 16, seq // 4 % 4, seq % 4
    xh, c = mp // 2, mp % 2

    kv_mine = lax.dynamic_slice_in_dim(w_keyval, 256 * c, 256, 1)
    kv_other = fetch(lax.dynamic_slice_in_dim(w_keyval, 256 * (1 - c), 256, 1), c=1)
    kv18 = jnp.where(
        c == 0,
        jnp.concatenate([kv_mine, kv_other], axis=0),
        jnp.concatenate([kv_other, kv_mine], axis=0),
    )
    short = jnp.pad(jnp.stack([query_gain, key_gain], axis=1), ((0, 28), (0, 0)))
    gains = jnp.stack([attn_pre_gain, attn_post_gain, ffn_pre_gain, ffn_post_gain], axis=1)
    gains = jnp.pad(jnp.concatenate([gains, short], axis=1), ((0, 0), (0, 122)))
    parcel = jnp.concatenate([w_query, gains, w_out.T, kv18.reshape(36, 128)], axis=1)
    half = fetch_line(lax.dynamic_slice_in_dim(tokens, 256 * c, 256, 0), -4)
    parcels = [
        [parcel, fetch(parcel, xh=1)],
        [fetch(parcel, xl=1), fetch(parcel, xl=1, xh=1)],
    ]
    parcels, half = lax.optimization_barrier((parcels, half))

    def kv36(pair):
        own, far = pair[0][:, 640:].reshape(18, 256), pair[1][:, 640:].reshape(18, 256)
        return jnp.where(
            xh == 0, jnp.concatenate([own, far], axis=0), jnp.concatenate([far, own], axis=0)
        )

    block_a = jnp.concatenate(
        [jnp.concatenate([p[0][:, :256], p[1][:, :256], p[0][:, 256:384]], axis=1) for p in parcels],
        axis=0,
    )
    block_b = jnp.concatenate(
        [jnp.concatenate([kv36(p), p[0][:, 384:640], p[1][:, 384:640]], axis=1) for p in parcels],
        axis=0,
    )
    part_a, part_b = gather_grids(block_a, block_b)
    part_ao = fetch(part_a[:, :512], c=1)
    part_bo = fetch(part_b, c=1)

    units = w_down.shape[0]
    ffn_own = jnp.stack([w_gate, w_up, w_down.T])
    ffn_own = jnp.pad(ffn_own, ((0, 0), (0, 0), (0, 2 * CUT - units)))
    ffn_own = jnp.stack(
        [
            jnp.concatenate([ffn_own[k, :, half * CUT : half * CUT + CUT] for k in range(3)], axis=1)
            for half in range(2)
        ]
    )
    ffn_own, block_a = lax.optimization_barrier((ffn_own, block_a))
    ffn_pair = jnp.concatenate([ffn_own, fetch(ffn_own, xl=1)], axis=1)
    ffn_pair, part_a, part_b = lax.optimization_barrier((ffn_pair, part_a, part_b))
    part_fa, part_fb = gather_grids(ffn_pair[0], ffn_pair[1])

    half_other = fetch(half, c=1)
    before = jnp.where(
        c == 0,
        jnp.concatenate([half, half_other], axis=0),
        jnp.concatenate([half_other, half], axis=0),
    )
    rows = lax.dynamic_slice_in_dim(jnp.concatenate([before, tokens], axis=0), ROWS * mp, KEYS, 0)
    column = jnp.arange(D, dtype=jnp.int32)
    zr, yr, xr, place = column // 288, column // 72 % 4, column // 36 % 2, column % 36
    owner = (xl ^ xr) * 16 + (z + zr) % 4 * 4 + (y + yr) % 4
    order = (column[:, None] == (owner * 36 + place)[None, :]).astype(bf16)
    short_owner = jnp.where(place < 8, owner * 8 + place, -1)
    short_order = (short_owner[:, None] == jnp.arange(HD, dtype=jnp.int32)[None, :]).astype(bf16)
    x_keys = dot(rows, order).astype(bf16).astype(f32)
    x = x_keys[WINDOW:]
    e_out = dot(lax.dynamic_slice_in_dim(grad_out, ROWS * mp, ROWS, 0), order).astype(bf16).astype(f32)
    r_keys = inverse_rms(x_keys)

    gain_cols = part_a[:, 512:]
    gain_rows = gain_cols[:, :8].T.astype(f32)
    pre_gain, post_gain, ffn_pre, ffn_post = (gain_rows[k : k + 1] for k in range(4))
    short_rows = dot_tn(gain_cols, short_order)
    qnorm_gain, knorm_gain = short_rows[4:5], short_rows[5:6]

    first_pos = seq % SEQ_BLOCKS * 512 + ROWS * mp
    positions = (first_pos - WINDOW + jnp.arange(KEYS, dtype=jnp.int32)).astype(f32)
    exponent = jnp.arange(HD // 2, dtype=f32) * (-2.0 / HD)
    angle = positions[:, None] * jnp.power(10000.0, exponent)[None, :]
    cosine, sine = jnp.cos(angle), jnp.sin(angle)
    cos_q, sin_q = cosine[WINDOW:], sine[WINDOW:]
    xn_keys = (x_keys * r_keys * pre_gain).astype(bf16)
    xn = xn_keys[WINDOW:]
    q_raw = [dot(xn, part_a[:, :512]), dot(xn, part_ao)]
    q_raw = jnp.stack([q_raw[h // 2][:, h % 2 * HD : h % 2 * HD + HD] for h in range(4)])
    kv_here, kv_there = dot(xn_keys, part_b[:, :HD]), dot(xn_keys, part_bo[:, :HD])
    key_raw = jnp.where(c == 0, kv_here, kv_there)
    values = jnp.where(c == 0, kv_there, kv_here).astype(bf16)
    r_q, r_k = inverse_rms(q_raw), inverse_rms(key_raw)
    query = rotary(q_raw * r_q * qnorm_gain, cos_q, sin_q).astype(bf16).reshape(4 * ROWS, HD)
    keys = rotary(key_raw * r_k * knorm_gain, cosine, sine).astype(bf16)
    row_ids = jnp.arange(ROWS, dtype=jnp.int32)[:, None]
    key_ids = jnp.arange(KEYS, dtype=jnp.int32)[None, :]
    allowed = (key_ids > row_ids) & (key_ids <= row_ids + WINDOW) & (key_ids + first_pos >= WINDOW)
    score = dot_nt(query, keys).reshape(4, ROWS, KEYS) * SCALE
    score = jnp.where(allowed[None], score, MASKED)
    peak = jnp.max(score, axis=-1, keepdims=True)
    weight = jnp.exp(score - peak)
    prob = weight / jnp.sum(weight, axis=-1, keepdims=True)
    prob_low = prob.astype(bf16).reshape(4 * ROWS, KEYS)
    att = dot(prob_low, values).astype(bf16).reshape(4, ROWS, HD)
    att = jnp.concatenate([att[h] for h in range(4)], axis=1)
    out_own, out_other = part_b[:, HD:], part_bo[:, HD:]
    branch = dot_nt(att[:, :512], out_own) + dot_nt(att[:, 512:], out_other)
    r_branch = inverse_rms(branch)
    mid = x + branch * r_branch * post_gain
    r_mid = inverse_rms(mid)
    hn_rows = (mid * r_mid * ffn_pre).astype(bf16)

    hn = gather_rows(hn_rows)
    gate_a, up_a, partial = ffn_forward(hn, part_fa, None)
    gate_b, up_b, partial = ffn_forward(hn, part_fb, partial)
    ffn = scatter_rows(partial)
    r_ffn = inverse_rms(ffn)
    output_rows = (mid + ffn * r_ffn * ffn_post).astype(bf16)
    d_ffn_rows, grad_ffn_post = norm_back(ffn, r_ffn, ffn_post, e_out)
    d_ffn = gather_rows(d_ffn_rows.astype(bf16))
    grads_a, partial = ffn_backward(d_ffn, part_fa, gate_a, up_a, None)
    grads_b, partial = ffn_backward(d_ffn, part_fb, gate_b, up_b, partial)
    d_hn = scatter_rows(partial)
    g_a, g_b = ffn_weights(hn, d_ffn, grads_a, 0), ffn_weights(hn, d_ffn, grads_b, 1)
    halves = halves_out(g_a, "y"), halves_out(g_b, "z")

    d_mid, grad_ffn_pre = norm_back(mid, r_mid, ffn_pre, d_hn)
    d_mid = d_mid + e_out
    d_branch, grad_post = norm_back(branch, r_branch, post_gain, d_mid)
    d_branch = d_branch.astype(bf16)
    d_att = [dot(d_branch, out_own), dot(d_branch, out_other)]
    d_att = jnp.stack([d_att[h // 2][:, h % 2 * HD : h % 2 * HD + HD] for h in range(4)])
    d_att = d_att.astype(bf16).reshape(4 * ROWS, HD)
    d_att, halves = lax.optimization_barrier((d_att, halves))
    sides = sides_out(g_a, halves[0], "y"), sides_out(g_b, halves[1], "z")
    d_prob = dot_nt(d_att, values).reshape(4, ROWS, KEYS)
    delta = jnp.sum(prob * d_prob, axis=-1, keepdims=True)
    d_score = (prob * (d_prob - delta)).astype(bf16).reshape(4 * ROWS, KEYS)
    d_query = dot(d_score, keys).reshape(4, ROWS, HD) * SCALE
    d_kv = jnp.concatenate(
        [dot_tn(d_score, query) * SCALE, dot_tn(prob_low, d_att)], axis=1
    ).reshape(5, ROWS, 2 * HD)
    d_kv_low = d_kv[:4].astype(bf16)
    d_kv_low, sides = lax.optimization_barrier((d_kv_low, sides))
    d_kv = add(d_kv[4], *[fetch_line(d_kv_low[k], 4 - k) for k in range(4)])
    line_a, line_b = add(g_a[0], *sides[0]).astype(bf16), add(g_b[0], *sides[1]).astype(bf16)
    g_ffn = jnp.stack(
        [
            scatter_small([line_a[k] for k in range(4)], "z"),
            scatter_small([line_b[k] for k in range(4)], "y"),
        ]
    )
    d_key = rotary(d_kv[:, :HD], cos_q, -sin_q)
    d_key_raw, grad_key_gain = norm_back(key_raw[WINDOW:], r_k[WINDOW:], knorm_gain, d_key)
    d_key_raw = d_key_raw.astype(bf16)
    d_value = d_kv[:, HD:].astype(bf16)
    d_here = jnp.where(c == 0, d_key_raw, d_value)
    d_there = jnp.where(c == 0, d_value, d_key_raw)
    d_q_raw, grad_query_gain = norm_back(q_raw, r_q, qnorm_gain, rotary(d_query, cos_q, -sin_q))
    d_q_raw = d_q_raw.astype(bf16)
    d_q_own = jnp.concatenate([d_q_raw[0], d_q_raw[1]], axis=1)
    d_q_other = jnp.concatenate([d_q_raw[2], d_q_raw[3]], axis=1)
    d_xn = (
        dot_nt(d_q_own, part_a[:, :512])
        + dot_nt(d_q_other, part_ao)
        + dot_nt(d_here, part_b[:, :HD])
        + dot_nt(d_there, part_bo[:, :HD])
    )
    d_x, grad_pre = norm_back(x, r_keys[WINDOW:], pre_gain, d_xn)
    d_tokens = (d_mid + d_x).astype(bf16)

    finished = [dot_nt(v, order).astype(bf16) for v in (output_rows, d_tokens)]
    finished = in_order(gather_rows(jnp.concatenate(finished, axis=1)), xh, c)
    output, grad_tokens = finished[:, :D], finished[:, D:]

    short_grads = dot_nt(jnp.stack([grad_query_gain, grad_key_gain]).astype(bf16), short_order)
    gain_grads = jnp.concatenate(
        [jnp.stack([grad_pre, grad_post, grad_ffn_pre, grad_ffn_post]), short_grads]
    )
    gain_grads = jnp.pad(gain_grads, ((0, 2), (0, 0))).T.astype(bf16)
    gain_grads = jnp.pad(gain_grads, ((0, 0), (0, 120)))
    own_a = jnp.concatenate([dot_tn(xn, d_q_own).astype(bf16), gain_grads], axis=1)
    other_a = jnp.concatenate([dot_tn(xn, d_q_other).astype(bf16), gain_grads], axis=1)
    own_b = jnp.concatenate([dot_tn(xn, d_here), dot_tn(d_branch, att[:, :512])], axis=1)
    other_b = jnp.concatenate([dot_tn(xn, d_there), dot_tn(d_branch, att[:, 512:])], axis=1)
    g_ffn = add(g_ffn[:, :36], fetch(g_ffn[:, 36:].astype(bf16), xl=1))
    g_ffn = [
        jnp.concatenate([g_ffn[0, :, at : at + CUT], g_ffn[1, :, at : at + units - CUT]], axis=1)
        for at in (0, CUT, 2 * CUT)
    ]
    sum_a = add(own_a, fetch(other_a, c=1)).astype(bf16)
    sum_b = add(own_b, fetch(other_b.astype(bf16), c=1)).astype(bf16)
    sum_a, sum_b = blocks_of([sum_a], 0), blocks_of([sum_b], 1)
    halves = halves_out(sum_a, "y"), halves_out(sum_b, "z")
    halves = lax.optimization_barrier(halves)
    sides = sides_out(sum_a, halves[0], "y"), sides_out(sum_b, halves[1], "z")
    sides = lax.optimization_barrier(sides)
    line_a, line_b = add(sum_a[0], *sides[0]).astype(bf16), add(sum_b[0], *sides[1]).astype(bf16)
    sum_a = scatter_small([line_a[k] for k in range(4)], "z").astype(bf16)
    sum_b = scatter_small([line_b[k] for k in range(4)], "y").astype(bf16)

    def parcel_back(xr_, xhr):
        a, b = sum_a[36 * xr_ : 36 * xr_ + 36], sum_b[36 * xr_ : 36 * xr_ + 36]
        kv = jnp.where(xh ^ xhr == 0, b[:18, :HD], b[18:, :HD]).reshape(36, 128)
        return jnp.concatenate(
            [a[:, 256 * xhr : 256 * xhr + 256], a[:, 512:], b[:, 256 + 256 * xhr : 512 + 256 * xhr], kv],
            axis=1,
        )

    total = add(
        parcel_back(0, 0),
        fetch(parcel_back(0, 1), xh=1),
        fetch(parcel_back(1, 0), xl=1),
        fetch(parcel_back(1, 1), xl=1, xh=1),
    )
    g_kv = total[:, 640:].reshape(18, 256)
    g_kv_here = jnp.where(c == 0, g_kv[:9], g_kv[9:])
    g_kv_away = fetch(jnp.where(c == 0, g_kv[9:], g_kv[:9]).astype(bf16), c=1).astype(f32)
    g_keyval = jnp.where(
        c == 0,
        jnp.concatenate([g_kv_here, g_kv_away], axis=1),
        jnp.concatenate([g_kv_away, g_kv_here], axis=1),
    )
    g_gains = total[:, 256:264].T
    return (
        output,
        grad_tokens,
        g_gains[0],
        total[:, :256],
        g_gains[4, :8],
        g_gains[5, :8],
        g_keyval,
        total[:, 384:640].T,
        g_gains[1],
        g_gains[2],
        g_ffn[0],
        g_ffn[1],
        g_ffn[2].T,
        g_gains[3],
    )


def solution(mesh):
    row, vector, weight, weight_t = P("seq", None), P("seq"), P("seq", "mp"), P("mp", "seq")
    keyval = P(("seq", "mp"), None)
    return jax.shard_map(
        per_device,
        mesh=mesh,
        in_specs=(row, row, vector, weight, vector, vector, keyval, weight_t)
        + (vector, vector, weight, weight, weight_t, vector),
        out_specs=(row, row, vector, weight, vector, vector, keyval, weight_t)
        + (vector, vector, weight, weight, weight_t, vector),
        check_vma=False,
    )
```

```python
import jax
import jax.numpy as jnp
from jax import lax
from jax.experimental import pallas as pl
from jax.experimental.pallas import tpu as pltpu
from jax.sharding import PartitionSpec as P

D = 1152
HD = 256
WINDOW = 512
SEQ_BLOCKS = 8
ROWS = 128
KEYS = ROWS + WINDOW
EPS = 1e-06
SCALE = 0.0625
MASKED = -1e30
SIZES = {"xl": 2, "z": 4, "y": 4, "xh": 2, "c": 2}
CUT = 896

bf16 = jnp.bfloat16
f32 = jnp.float32


def coords(n):
    mp, s = n % 4, n // 4
    return {"xl": s // 16, "z": s // 4 % 4, "y": s % 4, "xh": mp // 2, "c": mp % 2}


def flat(at):
    return ((at["xl"] * 4 + at["z"]) * 4 + at["y"]) * 4 + at["xh"] * 2 + at["c"]


def fetch(x, **delta):
    pairs = []
    for n in range(128):
        at = coords(n)
        for axis, by in delta.items():
            at[axis] = (at[axis] + by) % SIZES[axis]
        pairs.append((flat(at), n))
    return lax.ppermute(x, ("seq", "mp"), pairs)


def fetch_line(x, by):
    pairs = [(n + by, n) for n in range(128) if 0 <= n + by < 128]
    return lax.ppermute(x, ("seq", "mp"), pairs)


def gather_small(x, axis):
    return [x] + [fetch(x, **{axis: k}) for k in (1, 2, 3)]


def gather_big(x, axis):
    one = fetch(x, **{axis: 1})
    three = fetch(x, **{axis: 3})
    two = [fetch(one[:2], **{axis: 1}), fetch(three[2:], **{axis: 3})]
    return [x, one, jnp.concatenate(two, axis=0), three]


def gather_lines(a, b):
    return lax.optimization_barrier((gather_small(a, "z"), gather_small(b, "y")))


def gather_grids(line_a, line_b):
    grid_a = jnp.stack(gather_big(jnp.stack(line_a), "y"), axis=1)
    grid_b = jnp.stack(gather_big(jnp.stack(line_b), "z"), axis=0)
    return grid_a.reshape(D, grid_a.shape[-1]), grid_b.reshape(D, grid_b.shape[-1])


def add(*terms):
    total = terms[0].astype(f32)
    for term in terms[1:]:
        total = total + term.astype(f32)
    return total


def scatter_small(blocks, axis):
    return add(blocks[0], *[fetch(blocks[k], **{axis: 4 - k}) for k in (1, 2, 3)])


def blocks_of(parts, route):
    grids = [part.reshape(4, 4, 72, part.shape[-1]) for part in parts]
    return [
        jnp.concatenate([grid[:, k] if route == 0 else grid[k] for grid in grids], axis=-1)
        for k in range(4)
    ]


def halves_out(blocks, axis):
    return fetch(blocks[2][:2], **{axis: 3}), fetch(blocks[2][2:], **{axis: 1})


def sides_out(blocks, halves, axis):
    one = jnp.concatenate([add(blocks[1][:2], halves[0]).astype(bf16), blocks[1][2:]], axis=0)
    three = jnp.concatenate([blocks[3][:2], add(blocks[3][2:], halves[1]).astype(bf16)], axis=0)
    return fetch(one, **{axis: 3}), fetch(three, **{axis: 1})


def gather_rows(x):
    core = fetch(x, c=1)
    far = fetch(x, xh=1)
    return jnp.concatenate([x, core, far, fetch(far, c=1)], axis=0)


def scatter_rows(x):
    got = [fetch(x[ROWS : 2 * ROWS], c=1), fetch(x[3 * ROWS :], c=1)]
    far = add(x[2 * ROWS : 3 * ROWS], got[1]).astype(bf16)
    return add(x[:ROWS], got[0], fetch(far, xh=1))


def in_order(rows, xh, c):
    grid = rows.reshape(2, 2, ROWS, rows.shape[-1])
    grid = jnp.where(xh == 0, grid, grid[::-1])
    return jnp.where(c == 0, grid, grid[:, ::-1]).reshape(rows.shape)


def dot(a, b):
    return jnp.dot(a, b, preferred_element_type=f32)


def dot_nt(a, b):
    return lax.dot_general(a, b, (((1,), (1,)), ((), ())), preferred_element_type=f32)


def dot_tn(a, b):
    return lax.dot_general(a, b, (((0,), (0,)), ((), ())), preferred_element_type=f32)


def inverse_rms(v):
    return lax.rsqrt(jnp.mean(v * v, axis=-1, keepdims=True) + EPS)


def norm_back(v, r, g, e):
    ev = e * v
    inner = jnp.mean(g * ev, axis=-1, keepdims=True)
    gain_axes = tuple(range(v.ndim - 1))
    return r * (g * e) - v * (r * r * r * inner), jnp.sum(ev * r, axis=gain_axes)


def rotary(v, cosine, sine):
    former, latter = v[..., :128], v[..., 128:]
    return jnp.concatenate([former * cosine - latter * sine, latter * cosine + former * sine], axis=-1)


def gelu_tanh(v):
    return 0.5 * v * (1.0 + jnp.tanh(0.7978845608028654 * (v + 0.044715 * v * v * v)))


def gated_hidden(gate_in, up_in):
    return gelu_tanh(gate_in) * up_in


def in_vmem(count):
    return [pl.BlockSpec(memory_space=pltpu.VMEM)] * count


def forward_kernel(hn_ref, w_ref, prior_ref, gate_ref, up_ref, sum_ref):
    hn = hn_ref[...]
    gate = dot(hn, w_ref[:, :CUT])
    up = dot(hn, w_ref[:, CUT : 2 * CUT])
    hidden = gated_hidden(gate, up).astype(bf16)
    gate_ref[...] = gate.astype(bf16)
    up_ref[...] = up.astype(bf16)
    total = dot_nt(hidden, w_ref[:, 2 * CUT :])
    if prior_ref is not None:
        total = total + prior_ref[...]
    sum_ref[...] = total.astype(sum_ref.dtype)


def ffn_forward(hn, w, prior):
    first = prior is None
    rows = hn.shape[0]
    kernel = (lambda a, b, *out: forward_kernel(a, b, None, *out)) if first else forward_kernel
    args = (hn, w) if first else (hn, w, prior)
    return pl.pallas_call(
        kernel,
        out_shape=(
            jax.ShapeDtypeStruct((rows, CUT), bf16),
            jax.ShapeDtypeStruct((rows, CUT), bf16),
            jax.ShapeDtypeStruct((rows, D), f32 if first else bf16),
        ),
        in_specs=in_vmem(len(args)),
        out_specs=tuple(in_vmem(3)),
        compiler_params=pltpu.CompilerParams(vmem_limit_bytes=36 * 2**20),
        cost_estimate=pl.CostEstimate(
            flops=6 * rows * D * CUT, bytes_accessed=12 * 2**20, transcendentals=rows * CUT
        ),
    )(*args)


def backward_kernel(d_ffn_ref, w_ref, gate_ref, up_ref, prior_ref, grads_ref, sum_ref):
    d_hidden = dot(d_ffn_ref[...], w_ref[:, 2 * CUT :])
    gate, up = gate_ref[...].astype(f32), up_ref[...].astype(f32)
    square = gate * gate
    tanh = jnp.tanh(0.7978845608028654 * (gate + 0.044715 * square * gate))
    half = 0.5 * (1.0 + tanh)
    gelu = gate * half
    slope = half + 0.5 * gate * (1.0 - tanh * tanh) * (
        0.7978845608028654 * (1.0 + 3 * 0.044715 * square)
    )
    d_gate = (d_hidden * up * slope).astype(bf16)
    d_up = (d_hidden * gelu).astype(bf16)
    grads_ref[0] = d_gate
    grads_ref[1] = d_up
    grads_ref[2] = (gelu * up).astype(bf16)
    total = dot_nt(d_gate, w_ref[:, :CUT]) + dot_nt(d_up, w_ref[:, CUT : 2 * CUT])
    if prior_ref is not None:
        total = total + prior_ref[...]
    sum_ref[...] = total.astype(sum_ref.dtype)


def ffn_backward(d_ffn, w, gate, up, prior):
    first = prior is None
    rows = d_ffn.shape[0]
    kernel = (
        (lambda a, b, g, u, *out: backward_kernel(a, b, g, u, None, *out)) if first else backward_kernel
    )
    args = (d_ffn, w, gate, up) if first else (d_ffn, w, gate, up, prior)
    return pl.pallas_call(
        kernel,
        out_shape=(
            jax.ShapeDtypeStruct((3, rows, CUT), bf16),
            jax.ShapeDtypeStruct((rows, D), f32 if first else bf16),
        ),
        in_specs=in_vmem(len(args)),
        out_specs=tuple(in_vmem(2)),
        compiler_params=pltpu.CompilerParams(vmem_limit_bytes=36 * 2**20),
        cost_estimate=pl.CostEstimate(
            flops=6 * rows * D * CUT, bytes_accessed=14 * 2**20, transcendentals=rows * CUT
        ),
    )(*args)


def weights_kernel(route, hn_ref, d_ffn_ref, grads_ref, out_ref):
    def product(left_ref):
        total = dot_tn(left_ref[...], grads_ref[0]).astype(bf16)
        for zr in range(4):
            for yr in range(4):
                block = total[72 * (4 * zr + yr) : 72 * (4 * zr + yr) + 72]
                if route == 0:
                    out_ref[yr, zr] = block
                else:
                    out_ref[zr, yr] = block

    which = pl.program_id(0)

    @pl.when(which < 2)
    def _():
        product(hn_ref)

    @pl.when(which == 2)
    def _():
        product(d_ffn_ref)


def ffn_weights(hn, d_ffn, grads, route):
    rows = hn.shape[0]
    whole = pl.BlockSpec((rows, D), lambda j: (0, 0))
    return pl.pallas_call(
        lambda *refs: weights_kernel(route, *refs),
        grid=(3,),
        out_shape=jax.ShapeDtypeStruct((4, 4, 72, 3 * CUT), bf16),
        in_specs=[whole, whole, pl.BlockSpec((1, rows, CUT), lambda j: (j, 0, 0))],
        out_specs=pl.BlockSpec((4, 4, 72, CUT), lambda j: (0, 0, 0, j)),
        compiler_params=pltpu.CompilerParams(vmem_limit_bytes=36 * 2**20),
        cost_estimate=pl.CostEstimate(
            flops=6 * rows * D * CUT, bytes_accessed=12 * 2**20, transcendentals=0
        ),
    )(hn, d_ffn, grads)


def per_device(
    tokens,
    grad_out,
    attn_pre_gain,
    w_query,
    query_gain,
    key_gain,
    w_keyval,
    w_out,
    attn_post_gain,
    ffn_pre_gain,
    w_gate,
    w_up,
    w_down,
    ffn_post_gain,
):
    seq = lax.axis_index("seq")
    mp = lax.axis_index("mp")
    xl, z, y = seq // 16, seq // 4 % 4, seq % 4
    xh, c = mp // 2, mp % 2

    kv_mine = lax.dynamic_slice_in_dim(w_keyval, 256 * c, 256, 1)
    kv_other = fetch(lax.dynamic_slice_in_dim(w_keyval, 256 * (1 - c), 256, 1), c=1)
    kv18 = jnp.where(
        c == 0,
        jnp.concatenate([kv_mine, kv_other], axis=0),
        jnp.concatenate([kv_other, kv_mine], axis=0),
    )
    short = jnp.pad(jnp.stack([query_gain, key_gain], axis=1), ((0, 28), (0, 0)))
    gains = jnp.stack([attn_pre_gain, attn_post_gain, ffn_pre_gain, ffn_post_gain], axis=1)
    gains = jnp.pad(jnp.concatenate([gains, short], axis=1), ((0, 0), (0, 122)))
    parcel = jnp.concatenate([w_query, gains, w_out.T, kv18.reshape(36, 128)], axis=1)
    half = fetch_line(lax.dynamic_slice_in_dim(tokens, 256 * c, 256, 0), -4)
    parcels = [
        [parcel, fetch(parcel, xh=1)],
        [fetch(parcel, xl=1), fetch(parcel, xl=1, xh=1)],
    ]
    units = w_down.shape[0]
    ffn_own = jnp.stack([w_gate, w_up, w_down.T])
    ffn_own = jnp.pad(ffn_own, ((0, 0), (0, 0), (0, 2 * CUT - units)))
    ffn_own = jnp.stack(
        [
            jnp.concatenate([ffn_own[k, :, half * CUT : half * CUT + CUT] for k in range(3)], axis=1)
            for half in range(2)
        ]
    )
    ffn_away = fetch(ffn_own, xl=1)
    parcels, half, ffn_away = lax.optimization_barrier((parcels, half, ffn_away))
    ffn_pair = jnp.concatenate([ffn_own, ffn_away], axis=1)


    def kv36(pair):
        own, far = pair[0][:, 640:].reshape(18, 256), pair[1][:, 640:].reshape(18, 256)
        return jnp.where(
            xh == 0, jnp.concatenate([own, far], axis=0), jnp.concatenate([far, own], axis=0)
        )

    block_a = jnp.concatenate(
        [jnp.concatenate([p[0][:, :256], p[1][:, :256], p[0][:, 256:384]], axis=1) for p in parcels],
        axis=0,
    )
    block_b = jnp.concatenate(
        [jnp.concatenate([kv36(p), p[0][:, 384:640], p[1][:, 384:640]], axis=1) for p in parcels],
        axis=0,
    )
    line_a, line_b = gather_lines(
        jnp.concatenate([block_a, ffn_pair[0]], axis=1), jnp.concatenate([block_b, ffn_pair[1]], axis=1)
    )
    part_a, part_b = gather_grids([v[:, :640] for v in line_a], [v[:, :768] for v in line_b])
    part_ao = fetch(part_a[:, :512], c=1)
    part_bo = fetch(part_b, c=1)
    line_a, line_b, part_a, part_b = lax.optimization_barrier((line_a, line_b, part_a, part_b))
    part_fa, part_fb = gather_grids([v[:, 640:] for v in line_a], [v[:, 768:] for v in line_b])

    half_other = fetch(half, c=1)
    before = jnp.where(
        c == 0,
        jnp.concatenate([half, half_other], axis=0),
        jnp.concatenate([half_other, half], axis=0),
    )
    rows = lax.dynamic_slice_in_dim(jnp.concatenate([before, tokens], axis=0), ROWS * mp, KEYS, 0)
    column = jnp.arange(D, dtype=jnp.int32)
    zr, yr, xr, place = column // 288, column // 72 % 4, column // 36 % 2, column % 36
    owner = (xl ^ xr) * 16 + (z + zr) % 4 * 4 + (y + yr) % 4
    order = (column[:, None] == (owner * 36 + place)[None, :]).astype(bf16)
    short_owner = jnp.where(place < 8, owner * 8 + place, -1)
    short_order = (short_owner[:, None] == jnp.arange(HD, dtype=jnp.int32)[None, :]).astype(bf16)
    x_keys = dot(rows, order).astype(bf16).astype(f32)
    x = x_keys[WINDOW:]
    e_out = dot(lax.dynamic_slice_in_dim(grad_out, ROWS * mp, ROWS, 0), order).astype(bf16).astype(f32)
    r_keys = inverse_rms(x_keys)

    gain_cols = part_a[:, 512:]
    gain_rows = gain_cols[:, :8].T.astype(f32)
    pre_gain, post_gain, ffn_pre, ffn_post = (gain_rows[k : k + 1] for k in range(4))
    short_rows = dot_tn(gain_cols, short_order)
    qnorm_gain, knorm_gain = short_rows[4:5], short_rows[5:6]

    first_pos = seq % SEQ_BLOCKS * 512 + ROWS * mp
    positions = (first_pos - WINDOW + jnp.arange(KEYS, dtype=jnp.int32)).astype(f32)
    exponent = jnp.arange(HD // 2, dtype=f32) * (-2.0 / HD)
    angle = positions[:, None] * jnp.power(10000.0, exponent)[None, :]
    cosine, sine = jnp.cos(angle), jnp.sin(angle)
    cos_q, sin_q = cosine[WINDOW:], sine[WINDOW:]
    xn_keys = (x_keys * r_keys * pre_gain).astype(bf16)
    xn = xn_keys[WINDOW:]
    q_raw = [dot(xn, part_a[:, :512]), dot(xn, part_ao)]
    q_raw = jnp.stack([q_raw[h // 2][:, h % 2 * HD : h % 2 * HD + HD] for h in range(4)])
    kv_here, kv_there = dot(xn_keys, part_b[:, :HD]), dot(xn_keys, part_bo[:, :HD])
    key_raw = jnp.where(c == 0, kv_here, kv_there)
    values = jnp.where(c == 0, kv_there, kv_here).astype(bf16)
    r_q, r_k = inverse_rms(q_raw), inverse_rms(key_raw)
    query = rotary(q_raw * r_q * qnorm_gain, cos_q, sin_q).astype(bf16).reshape(4 * ROWS, HD)
    keys = rotary(key_raw * r_k * knorm_gain, cosine, sine).astype(bf16)
    row_ids = jnp.arange(ROWS, dtype=jnp.int32)[:, None]
    key_ids = jnp.arange(KEYS, dtype=jnp.int32)[None, :]
    allowed = (key_ids > row_ids) & (key_ids <= row_ids + WINDOW) & (key_ids + first_pos >= WINDOW)
    score = dot_nt(query, keys).reshape(4, ROWS, KEYS) * SCALE
    score = jnp.where(allowed[None], score, MASKED)
    peak = jnp.max(score, axis=-1, keepdims=True)
    weight = jnp.exp(score - peak)
    prob = weight / jnp.sum(weight, axis=-1, keepdims=True)
    prob_low = prob.astype(bf16).reshape(4 * ROWS, KEYS)
    att = dot(prob_low, values).astype(bf16).reshape(4, ROWS, HD)
    att = jnp.concatenate([att[h] for h in range(4)], axis=1)
    out_own, out_other = part_b[:, HD:], part_bo[:, HD:]
    branch = dot_nt(att[:, :512], out_own) + dot_nt(att[:, 512:], out_other)
    r_branch = inverse_rms(branch)
    mid = x + branch * r_branch * post_gain
    r_mid = inverse_rms(mid)
    hn_rows = (mid * r_mid * ffn_pre).astype(bf16)

    hn = gather_rows(hn_rows)
    gate_a, up_a, partial = ffn_forward(hn, part_fa, None)
    gate_b, up_b, partial = ffn_forward(hn, part_fb, partial)
    ffn = scatter_rows(partial)
    r_ffn = inverse_rms(ffn)
    output_rows = (mid + ffn * r_ffn * ffn_post).astype(bf16)
    d_ffn_rows, grad_ffn_post = norm_back(ffn, r_ffn, ffn_post, e_out)
    d_ffn = gather_rows(d_ffn_rows.astype(bf16))
    grads_a, partial = ffn_backward(d_ffn, part_fa, gate_a, up_a, None)
    grads_b, partial = ffn_backward(d_ffn, part_fb, gate_b, up_b, partial)
    d_hn = scatter_rows(partial)
    g_a, g_b = ffn_weights(hn, d_ffn, grads_a, 0), ffn_weights(hn, d_ffn, grads_b, 1)
    halves = halves_out(g_a, "y"), halves_out(g_b, "z")

    d_mid, grad_ffn_pre = norm_back(mid, r_mid, ffn_pre, d_hn)
    d_mid = d_mid + e_out
    d_branch, grad_post = norm_back(branch, r_branch, post_gain, d_mid)
    d_branch = d_branch.astype(bf16)
    d_att = [dot(d_branch, out_own), dot(d_branch, out_other)]
    d_att = jnp.stack([d_att[h // 2][:, h % 2 * HD : h % 2 * HD + HD] for h in range(4)])
    d_att = d_att.astype(bf16).reshape(4 * ROWS, HD)
    d_att, halves = lax.optimization_barrier((d_att, halves))
    sides = sides_out(g_a, halves[0], "y"), sides_out(g_b, halves[1], "z")
    d_prob = dot_nt(d_att, values).reshape(4, ROWS, KEYS)
    delta = jnp.sum(prob * d_prob, axis=-1, keepdims=True)
    d_score = (prob * (d_prob - delta)).astype(bf16).reshape(4 * ROWS, KEYS)
    d_query = dot(d_score, keys).reshape(4, ROWS, HD) * SCALE
    d_kv = jnp.concatenate(
        [dot_tn(d_score, query) * SCALE, dot_tn(prob_low, d_att)], axis=1
    ).reshape(5, ROWS, 2 * HD)
    d_kv_low = d_kv[:4].astype(bf16)
    d_kv = add(d_kv[4], *[fetch_line(d_kv_low[k], 4 - k) for k in range(4)])
    d_key = rotary(d_kv[:, :HD], cos_q, -sin_q)
    d_key_raw, grad_key_gain = norm_back(key_raw[WINDOW:], r_k[WINDOW:], knorm_gain, d_key)
    d_key_raw = d_key_raw.astype(bf16)
    d_value = d_kv[:, HD:].astype(bf16)
    d_here = jnp.where(c == 0, d_key_raw, d_value)
    d_there = jnp.where(c == 0, d_value, d_key_raw)
    d_q_raw, grad_query_gain = norm_back(q_raw, r_q, qnorm_gain, rotary(d_query, cos_q, -sin_q))
    d_q_raw = d_q_raw.astype(bf16)
    d_q_own = jnp.concatenate([d_q_raw[0], d_q_raw[1]], axis=1)
    d_q_other = jnp.concatenate([d_q_raw[2], d_q_raw[3]], axis=1)
    d_xn = (
        dot_nt(d_q_own, part_a[:, :512])
        + dot_nt(d_q_other, part_ao)
        + dot_nt(d_here, part_b[:, :HD])
        + dot_nt(d_there, part_bo[:, :HD])
    )
    d_x, grad_pre = norm_back(x, r_keys[WINDOW:], pre_gain, d_xn)
    d_tokens = (d_mid + d_x).astype(bf16)

    finished = [dot_nt(v, order).astype(bf16) for v in (output_rows, d_tokens)]
    finished = in_order(gather_rows(jnp.concatenate(finished, axis=1)), xh, c)
    output, grad_tokens = finished[:, :D], finished[:, D:]

    short_grads = dot_nt(jnp.stack([grad_query_gain, grad_key_gain]).astype(bf16), short_order)
    gain_grads = jnp.concatenate(
        [jnp.stack([grad_pre, grad_post, grad_ffn_pre, grad_ffn_post]), short_grads]
    )
    gain_grads = jnp.pad(gain_grads, ((0, 2), (0, 0))).T.astype(bf16)
    gain_grads = jnp.pad(gain_grads, ((0, 0), (0, 120)))
    own_a = jnp.concatenate([dot_tn(xn, d_q_own).astype(bf16), gain_grads], axis=1)
    other_a = jnp.concatenate([dot_tn(xn, d_q_other).astype(bf16), gain_grads], axis=1)
    own_b = jnp.concatenate([dot_tn(xn, d_here), dot_tn(d_branch, att[:, :512])], axis=1)
    other_b = jnp.concatenate([dot_tn(xn, d_there), dot_tn(d_branch, att[:, 512:])], axis=1)
    other_a, other_b, sides = lax.optimization_barrier((other_a, other_b.astype(bf16), sides))
    line_a, line_b = add(g_a[0], *sides[0]).astype(bf16), add(g_b[0], *sides[1]).astype(bf16)
    g_ffn = jnp.stack(
        [
            scatter_small([line_a[k] for k in range(4)], "z"),
            scatter_small([line_b[k] for k in range(4)], "y"),
        ]
    )
    g_ffn = add(g_ffn[:, :36], fetch(g_ffn[:, 36:].astype(bf16), xl=1))
    g_ffn = [
        jnp.concatenate([g_ffn[0, :, at : at + CUT], g_ffn[1, :, at : at + units - CUT]], axis=1)
        for at in (0, CUT, 2 * CUT)
    ]
    sum_a = add(own_a, fetch(other_a, c=1)).astype(bf16)
    sum_b = add(own_b, fetch(other_b, c=1)).astype(bf16)
    sum_a, sum_b = blocks_of([sum_a], 0), blocks_of([sum_b], 1)
    halves = halves_out(sum_a, "y"), halves_out(sum_b, "z")
    halves = lax.optimization_barrier(halves)
    sides = sides_out(sum_a, halves[0], "y"), sides_out(sum_b, halves[1], "z")
    sides = lax.optimization_barrier(sides)
    line_a, line_b = add(sum_a[0], *sides[0]).astype(bf16), add(sum_b[0], *sides[1]).astype(bf16)
    sum_a = scatter_small([line_a[k] for k in range(4)], "z").astype(bf16)
    sum_b = scatter_small([line_b[k] for k in range(4)], "y").astype(bf16)

    def parcel_back(xr_, xhr):
        a, b = sum_a[36 * xr_ : 36 * xr_ + 36], sum_b[36 * xr_ : 36 * xr_ + 36]
        kv = jnp.where(xh ^ xhr == 0, b[:18, :HD], b[18:, :HD]).reshape(36, 128)
        return jnp.concatenate(
            [a[:, 256 * xhr : 256 * xhr + 256], a[:, 512:], b[:, 256 + 256 * xhr : 512 + 256 * xhr], kv],
            axis=1,
        )

    total = add(
        parcel_back(0, 0),
        fetch(parcel_back(0, 1), xh=1),
        fetch(parcel_back(1, 0), xl=1),
        fetch(parcel_back(1, 1), xl=1, xh=1),
    )
    g_kv = total[:, 640:].reshape(18, 256)
    g_kv_here = jnp.where(c == 0, g_kv[:9], g_kv[9:])
    g_kv_away = fetch(jnp.where(c == 0, g_kv[9:], g_kv[:9]).astype(bf16), c=1).astype(f32)
    g_keyval = jnp.where(
        c == 0,
        jnp.concatenate([g_kv_here, g_kv_away], axis=1),
        jnp.concatenate([g_kv_away, g_kv_here], axis=1),
    )
    g_gains = total[:, 256:264].T
    return (
        output,
        grad_tokens,
        g_gains[0],
        total[:, :256],
        g_gains[4, :8],
        g_gains[5, :8],
        g_keyval,
        total[:, 384:640].T,
        g_gains[1],
        g_gains[2],
        g_ffn[0],
        g_ffn[1],
        g_ffn[2].T,
        g_gains[3],
    )


def solution(mesh):
    row, vector, weight, weight_t = P("seq", None), P("seq"), P("seq", "mp"), P("mp", "seq")
    keyval = P(("seq", "mp"), None)
    return jax.shard_map(
        per_device,
        mesh=mesh,
        in_specs=(row, row, vector, weight, vector, vector, keyval, weight_t)
        + (vector, vector, weight, weight, weight_t, vector),
        out_specs=(row, row, vector, weight, vector, vector, keyval, weight_t)
        + (vector, vector, weight, weight, weight_t, vector),
        check_vma=False,
    )
```

```python
import jax
import jax.numpy as jnp
from jax import lax
from jax.experimental import pallas as pl
from jax.experimental.pallas import tpu as pltpu
from jax.sharding import PartitionSpec as P

D = 1152
HD = 256
WINDOW = 512
SEQ_BLOCKS = 8
ROWS = 128
KEYS = ROWS + WINDOW
EPS = 1e-06
SCALE = 0.0625
MASKED = -1e30
SIZES = {"xl": 2, "z": 4, "y": 4, "xh": 2, "c": 2}
CUT = 896

bf16 = jnp.bfloat16
f32 = jnp.float32


def coords(n):
    mp, s = n % 4, n // 4
    return {"xl": s // 16, "z": s // 4 % 4, "y": s % 4, "xh": mp // 2, "c": mp % 2}


def flat(at):
    return ((at["xl"] * 4 + at["z"]) * 4 + at["y"]) * 4 + at["xh"] * 2 + at["c"]


def fetch(x, **delta):
    pairs = []
    for n in range(128):
        at = coords(n)
        for axis, by in delta.items():
            at[axis] = (at[axis] + by) % SIZES[axis]
        pairs.append((flat(at), n))
    return lax.ppermute(x, ("seq", "mp"), pairs)


def fetch_line(x, by):
    pairs = [(n + by, n) for n in range(128) if 0 <= n + by < 128]
    return lax.ppermute(x, ("seq", "mp"), pairs)


def gather_small(x, axis):
    return [x] + [fetch(x, **{axis: k}) for k in (1, 2, 3)]


def gather_big(x, axis):
    one = fetch(x, **{axis: 1})
    three = fetch(x, **{axis: 3})
    two = [fetch(one[:2], **{axis: 1}), fetch(three[2:], **{axis: 3})]
    return [x, one, jnp.concatenate(two, axis=0), three]


def gather_onward(x, axis):
    one = fetch(x, **{axis: 1})
    return [x, one, fetch(one, **{axis: 1}), fetch(x, **{axis: 3})]


def gather_grids(a, b, first):
    line_a, line_b = lax.optimization_barrier((first(a, "z"), first(b, "y")))
    grid_a = jnp.stack(gather_big(jnp.stack(line_a), "y"), axis=1)
    grid_b = jnp.stack(gather_big(jnp.stack(line_b), "z"), axis=0)
    return grid_a.reshape(D, a.shape[-1]), grid_b.reshape(D, b.shape[-1])


def add(*terms):
    total = terms[0].astype(f32)
    for term in terms[1:]:
        total = total + term.astype(f32)
    return total


def scatter_small(blocks, axis):
    return add(blocks[0], *[fetch(blocks[k], **{axis: 4 - k}) for k in (1, 2, 3)])


def blocks_of(parts, route):
    grids = [part.reshape(4, 4, 72, part.shape[-1]) for part in parts]
    return [
        jnp.concatenate([grid[:, k] if route == 0 else grid[k] for grid in grids], axis=-1)
        for k in range(4)
    ]


def halves_out(blocks, axis):
    return fetch(blocks[2][:2], **{axis: 3}), fetch(blocks[2][2:], **{axis: 1})


def sides_out(blocks, halves, axis):
    one = jnp.concatenate([add(blocks[1][:2], halves[0]).astype(bf16), blocks[1][2:]], axis=0)
    three = jnp.concatenate([blocks[3][:2], add(blocks[3][2:], halves[1]).astype(bf16)], axis=0)
    return fetch(one, **{axis: 3}), fetch(three, **{axis: 1})


def gather_rows(x):
    core = fetch(x, c=1)
    far = fetch(x, xh=1)
    return jnp.concatenate([x, core, far, fetch(far, c=1)], axis=0)


def scatter_rows(x):
    got = [fetch(x[ROWS : 2 * ROWS], c=1), fetch(x[3 * ROWS :], c=1)]
    far = add(x[2 * ROWS : 3 * ROWS], got[1]).astype(bf16)
    return add(x[:ROWS], got[0], fetch(far, xh=1))


def in_order(rows, xh, c):
    grid = rows.reshape(2, 2, ROWS, rows.shape[-1])
    grid = jnp.where(xh == 0, grid, grid[::-1])
    return jnp.where(c == 0, grid, grid[:, ::-1]).reshape(rows.shape)


def dot(a, b):
    return jnp.dot(a, b, preferred_element_type=f32)


def dot_nt(a, b):
    return lax.dot_general(a, b, (((1,), (1,)), ((), ())), preferred_element_type=f32)


def dot_tn(a, b):
    return lax.dot_general(a, b, (((0,), (0,)), ((), ())), preferred_element_type=f32)


def inverse_rms(v):
    return lax.rsqrt(jnp.mean(v * v, axis=-1, keepdims=True) + EPS)


def norm_back(v, r, g, e):
    ev = e * v
    inner = jnp.mean(g * ev, axis=-1, keepdims=True)
    gain_axes = tuple(range(v.ndim - 1))
    return r * (g * e) - v * (r * r * r * inner), jnp.sum(ev * r, axis=gain_axes)


def rotary(v, cosine, sine):
    former, latter = v[..., :128], v[..., 128:]
    return jnp.concatenate([former * cosine - latter * sine, latter * cosine + former * sine], axis=-1)


def gelu_tanh(v):
    return 0.5 * v * (1.0 + jnp.tanh(0.7978845608028654 * (v + 0.044715 * v * v * v)))


def gated_hidden(gate_in, up_in):
    return gelu_tanh(gate_in) * up_in


def in_vmem(count):
    return [pl.BlockSpec(memory_space=pltpu.VMEM)] * count


def forward_kernel(hn_ref, w_ref, prior_ref, gate_ref, up_ref, sum_ref):
    hn = hn_ref[...]
    gate = dot(hn, w_ref[:, :CUT])
    up = dot(hn, w_ref[:, CUT : 2 * CUT])
    hidden = gated_hidden(gate, up).astype(bf16)
    gate_ref[...] = gate.astype(bf16)
    up_ref[...] = up.astype(bf16)
    total = dot_nt(hidden, w_ref[:, 2 * CUT :])
    if prior_ref is not None:
        total = total + prior_ref[...]
    sum_ref[...] = total.astype(sum_ref.dtype)


def ffn_forward(hn, w, prior):
    first = prior is None
    rows = hn.shape[0]
    kernel = (lambda a, b, *out: forward_kernel(a, b, None, *out)) if first else forward_kernel
    args = (hn, w) if first else (hn, w, prior)
    return pl.pallas_call(
        kernel,
        out_shape=(
            jax.ShapeDtypeStruct((rows, CUT), bf16),
            jax.ShapeDtypeStruct((rows, CUT), bf16),
            jax.ShapeDtypeStruct((rows, D), f32 if first else bf16),
        ),
        in_specs=in_vmem(len(args)),
        out_specs=tuple(in_vmem(3)),
        compiler_params=pltpu.CompilerParams(vmem_limit_bytes=36 * 2**20),
        cost_estimate=pl.CostEstimate(
            flops=6 * rows * D * CUT, bytes_accessed=12 * 2**20, transcendentals=rows * CUT
        ),
    )(*args)


def backward_kernel(d_ffn_ref, w_ref, gate_ref, up_ref, prior_ref, grads_ref, sum_ref):
    d_hidden = dot(d_ffn_ref[...], w_ref[:, 2 * CUT :])
    gate, up = gate_ref[...].astype(f32), up_ref[...].astype(f32)
    square = gate * gate
    tanh = jnp.tanh(0.7978845608028654 * (gate + 0.044715 * square * gate))
    half = 0.5 * (1.0 + tanh)
    gelu = gate * half
    slope = half + 0.5 * gate * (1.0 - tanh * tanh) * (
        0.7978845608028654 * (1.0 + 3 * 0.044715 * square)
    )
    d_gate = (d_hidden * up * slope).astype(bf16)
    d_up = (d_hidden * gelu).astype(bf16)
    grads_ref[0] = d_gate
    grads_ref[1] = d_up
    grads_ref[2] = (gelu * up).astype(bf16)
    total = dot_nt(d_gate, w_ref[:, :CUT]) + dot_nt(d_up, w_ref[:, CUT : 2 * CUT])
    if prior_ref is not None:
        total = total + prior_ref[...]
    sum_ref[...] = total.astype(sum_ref.dtype)


def ffn_backward(d_ffn, w, gate, up, prior):
    first = prior is None
    rows = d_ffn.shape[0]
    kernel = (
        (lambda a, b, g, u, *out: backward_kernel(a, b, g, u, None, *out)) if first else backward_kernel
    )
    args = (d_ffn, w, gate, up) if first else (d_ffn, w, gate, up, prior)
    return pl.pallas_call(
        kernel,
        out_shape=(
            jax.ShapeDtypeStruct((3, rows, CUT), bf16),
            jax.ShapeDtypeStruct((rows, D), f32 if first else bf16),
        ),
        in_specs=in_vmem(len(args)),
        out_specs=tuple(in_vmem(2)),
        compiler_params=pltpu.CompilerParams(vmem_limit_bytes=36 * 2**20),
        cost_estimate=pl.CostEstimate(
            flops=6 * rows * D * CUT, bytes_accessed=14 * 2**20, transcendentals=rows * CUT
        ),
    )(*args)


def weights_kernel(route, hn_ref, d_ffn_ref, grads_ref, out_ref):
    def product(left_ref):
        total = dot_tn(left_ref[...], grads_ref[0]).astype(bf16)
        for zr in range(4):
            for yr in range(4):
                block = total[72 * (4 * zr + yr) : 72 * (4 * zr + yr) + 72]
                if route == 0:
                    out_ref[yr, zr] = block
                else:
                    out_ref[zr, yr] = block

    which = pl.program_id(0)

    @pl.when(which < 2)
    def _():
        product(hn_ref)

    @pl.when(which == 2)
    def _():
        product(d_ffn_ref)


def ffn_weights(hn, d_ffn, grads, route):
    rows = hn.shape[0]
    whole = pl.BlockSpec((rows, D), lambda j: (0, 0))
    return pl.pallas_call(
        lambda *refs: weights_kernel(route, *refs),
        grid=(3,),
        out_shape=jax.ShapeDtypeStruct((4, 4, 72, 3 * CUT), bf16),
        in_specs=[whole, whole, pl.BlockSpec((1, rows, CUT), lambda j: (j, 0, 0))],
        out_specs=pl.BlockSpec((4, 4, 72, CUT), lambda j: (0, 0, 0, j)),
        compiler_params=pltpu.CompilerParams(vmem_limit_bytes=36 * 2**20),
        cost_estimate=pl.CostEstimate(
            flops=6 * rows * D * CUT, bytes_accessed=12 * 2**20, transcendentals=0
        ),
    )(hn, d_ffn, grads)


def attention_weights_kernel(xn, d_branch, gains, *refs):
    sides, outs = refs[:6], refs[6:]
    for k in range(2):
        d_q, d_kv, att = sides[3 * k : 3 * k + 3]
        out_a, out_b = outs[2 * k : 2 * k + 2]
        out_a[:, :512] = dot_tn(xn[...], d_q[...]).astype(bf16)
        out_a[:, 512:] = gains[...]
        out_b[:, :HD] = dot_tn(xn[...], d_kv[...]).astype(bf16)
        out_b[:, HD:] = dot_tn(d_branch[...], att[...]).astype(bf16)


def attention_weights(xn, d_branch, gains, here, there):
    shapes = tuple(jax.ShapeDtypeStruct((D, n), bf16) for n in (640, 768, 640, 768))
    return pl.pallas_call(
        attention_weights_kernel,
        out_shape=shapes,
        in_specs=in_vmem(9),
        out_specs=tuple(in_vmem(4)),
        compiler_params=pltpu.CompilerParams(vmem_limit_bytes=24 * 2**20),
        cost_estimate=pl.CostEstimate(
            flops=2 * ROWS * D * 2560, bytes_accessed=8 * 2**20, transcendentals=0
        ),
    )(xn, d_branch, gains, *here, *there)


def per_device(
    tokens,
    grad_out,
    attn_pre_gain,
    w_query,
    query_gain,
    key_gain,
    w_keyval,
    w_out,
    attn_post_gain,
    ffn_pre_gain,
    w_gate,
    w_up,
    w_down,
    ffn_post_gain,
):
    seq = lax.axis_index("seq")
    mp = lax.axis_index("mp")
    xl, z, y = seq // 16, seq // 4 % 4, seq % 4
    xh, c = mp // 2, mp % 2

    kv_mine = lax.dynamic_slice_in_dim(w_keyval, 256 * c, 256, 1)
    kv_other = fetch(lax.dynamic_slice_in_dim(w_keyval, 256 * (1 - c), 256, 1), c=1)
    kv18 = jnp.where(
        c == 0,
        jnp.concatenate([kv_mine, kv_other], axis=0),
        jnp.concatenate([kv_other, kv_mine], axis=0),
    )
    short = jnp.pad(jnp.stack([query_gain, key_gain], axis=1), ((0, 28), (0, 0)))
    gains = jnp.stack([attn_pre_gain, attn_post_gain, ffn_pre_gain, ffn_post_gain], axis=1)
    gains = jnp.pad(jnp.concatenate([gains, short], axis=1), ((0, 0), (0, 122)))
    parcel = jnp.concatenate([w_query, gains, w_out.T, kv18.reshape(36, 128)], axis=1)
    half = fetch_line(lax.dynamic_slice_in_dim(tokens, 256 * c, 256, 0), -4)
    parcels = [
        [parcel, fetch(parcel, xh=1)],
        [fetch(parcel, xl=1), fetch(parcel, xl=1, xh=1)],
    ]
    parcels, half = lax.optimization_barrier((parcels, half))

    def kv36(pair):
        own, far = pair[0][:, 640:].reshape(18, 256), pair[1][:, 640:].reshape(18, 256)
        return jnp.where(
            xh == 0, jnp.concatenate([own, far], axis=0), jnp.concatenate([far, own], axis=0)
        )

    block_a = jnp.concatenate(
        [jnp.concatenate([p[0][:, :256], p[1][:, :256], p[0][:, 256:384]], axis=1) for p in parcels],
        axis=0,
    )
    block_b = jnp.concatenate(
        [jnp.concatenate([kv36(p), p[0][:, 384:640], p[1][:, 384:640]], axis=1) for p in parcels],
        axis=0,
    )
    part_a, part_b = gather_grids(block_a, block_b, gather_small)
    part_ao = fetch(part_a[:, :512], c=1)
    part_bo = fetch(part_b, c=1)

    units = w_down.shape[0]
    ffn_own = jnp.stack([w_gate, w_up, w_down.T])
    ffn_own = jnp.pad(ffn_own, ((0, 0), (0, 0), (0, 2 * CUT - units)))
    ffn_own = jnp.stack(
        [
            jnp.concatenate([ffn_own[k, :, half * CUT : half * CUT + CUT] for k in range(3)], axis=1)
            for half in range(2)
        ]
    )
    ffn_own, block_a = lax.optimization_barrier((ffn_own, block_a))
    ffn_pair = jnp.concatenate([ffn_own, fetch(ffn_own, xl=1)], axis=1)
    ffn_pair, part_a, part_b = lax.optimization_barrier((ffn_pair, part_a, part_b))
    part_fa, part_fb = gather_grids(ffn_pair[0], ffn_pair[1], gather_onward)

    half_other = fetch(half, c=1)
    before = jnp.where(
        c == 0,
        jnp.concatenate([half, half_other], axis=0),
        jnp.concatenate([half_other, half], axis=0),
    )
    rows = lax.dynamic_slice_in_dim(jnp.concatenate([before, tokens], axis=0), ROWS * mp, KEYS, 0)
    column = jnp.arange(D, dtype=jnp.int32)
    zr, yr, xr, place = column // 288, column // 72 % 4, column // 36 % 2, column % 36
    owner = (xl ^ xr) * 16 + (z + zr) % 4 * 4 + (y + yr) % 4
    order = (column[:, None] == (owner * 36 + place)[None, :]).astype(bf16)
    short_owner = jnp.where(place < 8, owner * 8 + place, -1)
    short_order = (short_owner[:, None] == jnp.arange(HD, dtype=jnp.int32)[None, :]).astype(bf16)
    x_keys = dot(rows, order).astype(bf16).astype(f32)
    x = x_keys[WINDOW:]
    e_out = dot(lax.dynamic_slice_in_dim(grad_out, ROWS * mp, ROWS, 0), order).astype(bf16).astype(f32)
    r_keys = inverse_rms(x_keys)

    gain_cols = part_a[:, 512:]
    gain_rows = gain_cols[:, :8].T.astype(f32)
    pre_gain, post_gain, ffn_pre, ffn_post = (gain_rows[k : k + 1] for k in range(4))
    short_rows = dot_tn(gain_cols, short_order)
    qnorm_gain, knorm_gain = short_rows[4:5], short_rows[5:6]

    first_pos = seq % SEQ_BLOCKS * 512 + ROWS * mp
    positions = (first_pos - WINDOW + jnp.arange(KEYS, dtype=jnp.int32)).astype(f32)
    exponent = jnp.arange(HD // 2, dtype=f32) * (-2.0 / HD)
    angle = positions[:, None] * jnp.power(10000.0, exponent)[None, :]
    cosine, sine = jnp.cos(angle), jnp.sin(angle)
    cos_q, sin_q = cosine[WINDOW:], sine[WINDOW:]
    xn_keys = (x_keys * r_keys * pre_gain).astype(bf16)
    xn = xn_keys[WINDOW:]
    q_raw = [dot(xn, part_a[:, :512]), dot(xn, part_ao)]
    q_raw = jnp.stack([q_raw[h // 2][:, h % 2 * HD : h % 2 * HD + HD] for h in range(4)])
    kv_here, kv_there = dot(xn_keys, part_b[:, :HD]), dot(xn_keys, part_bo[:, :HD])
    key_raw = jnp.where(c == 0, kv_here, kv_there)
    values = jnp.where(c == 0, kv_there, kv_here).astype(bf16)
    r_q, r_k = inverse_rms(q_raw), inverse_rms(key_raw)
    query = rotary(q_raw * r_q * qnorm_gain, cos_q, sin_q).astype(bf16).reshape(4 * ROWS, HD)
    keys = rotary(key_raw * r_k * knorm_gain, cosine, sine).astype(bf16)
    row_ids = jnp.arange(ROWS, dtype=jnp.int32)[:, None]
    key_ids = jnp.arange(KEYS, dtype=jnp.int32)[None, :]
    allowed = (key_ids > row_ids) & (key_ids <= row_ids + WINDOW) & (key_ids + first_pos >= WINDOW)
    score = dot_nt(query, keys).reshape(4, ROWS, KEYS) * SCALE
    score = jnp.where(allowed[None], score, MASKED)
    peak = jnp.max(score, axis=-1, keepdims=True)
    weight = jnp.exp(score - peak)
    prob = weight / jnp.sum(weight, axis=-1, keepdims=True)
    prob_low = prob.astype(bf16).reshape(4 * ROWS, KEYS)
    att = dot(prob_low, values).astype(bf16).reshape(4, ROWS, HD)
    att = jnp.concatenate([att[h] for h in range(4)], axis=1)
    out_own, out_other = part_b[:, HD:], part_bo[:, HD:]
    branch = dot_nt(att[:, :512], out_own) + dot_nt(att[:, 512:], out_other)
    r_branch = inverse_rms(branch)
    mid = x + branch * r_branch * post_gain
    r_mid = inverse_rms(mid)
    hn_rows = (mid * r_mid * ffn_pre).astype(bf16)

    hn = gather_rows(hn_rows)
    gate_a, up_a, partial = ffn_forward(hn, part_fa, None)
    gate_b, up_b, partial = ffn_forward(hn, part_fb, partial)
    ffn = scatter_rows(partial)
    r_ffn = inverse_rms(ffn)
    output_rows = (mid + ffn * r_ffn * ffn_post).astype(bf16)
    d_ffn_rows, grad_ffn_post = norm_back(ffn, r_ffn, ffn_post, e_out)
    d_ffn = gather_rows(d_ffn_rows.astype(bf16))
    grads_a, partial = ffn_backward(d_ffn, part_fa, gate_a, up_a, None)
    grads_b, partial = ffn_backward(d_ffn, part_fb, gate_b, up_b, partial)
    d_hn = scatter_rows(partial)
    g_a, g_b = ffn_weights(hn, d_ffn, grads_a, 0), ffn_weights(hn, d_ffn, grads_b, 1)
    halves = halves_out(g_a, "y"), halves_out(g_b, "z")

    d_mid, grad_ffn_pre = norm_back(mid, r_mid, ffn_pre, d_hn)
    d_mid = d_mid + e_out
    d_branch, grad_post = norm_back(branch, r_branch, post_gain, d_mid)
    d_branch = d_branch.astype(bf16)
    d_att = [dot(d_branch, out_own), dot(d_branch, out_other)]
    d_att = jnp.stack([d_att[h // 2][:, h % 2 * HD : h % 2 * HD + HD] for h in range(4)])
    d_att = d_att.astype(bf16).reshape(4 * ROWS, HD)
    d_att, halves = lax.optimization_barrier((d_att, halves))
    sides = sides_out(g_a, halves[0], "y"), sides_out(g_b, halves[1], "z")
    d_prob = dot_nt(d_att, values).reshape(4, ROWS, KEYS)
    delta = jnp.sum(prob * d_prob, axis=-1, keepdims=True)
    d_score = (prob * (d_prob - delta)).astype(bf16).reshape(4 * ROWS, KEYS)
    d_query = dot(d_score, keys).reshape(4, ROWS, HD) * SCALE
    d_kv = jnp.concatenate(
        [dot_tn(d_score, query) * SCALE, dot_tn(prob_low, d_att)], axis=1
    ).reshape(5, ROWS, 2 * HD)
    d_kv_low = d_kv[:4].astype(bf16)
    d_q_raw, grad_query_gain = norm_back(q_raw, r_q, qnorm_gain, rotary(d_query, cos_q, -sin_q))
    d_q_raw = d_q_raw.astype(bf16)
    d_q_own = jnp.concatenate([d_q_raw[0], d_q_raw[1]], axis=1)
    d_q_other = jnp.concatenate([d_q_raw[2], d_q_raw[3]], axis=1)
    out_rows = dot_nt(output_rows, order).astype(bf16)
    d_kv_low, sides, d_q_own, d_q_other, grad_query_gain, out_rows = lax.optimization_barrier(
        (d_kv_low, sides, d_q_own, d_q_other, grad_query_gain, out_rows)
    )
    ffn_sides = sides
    d_kv = add(d_kv[4], *[fetch_line(d_kv_low[k], 4 - k) for k in range(4)])
    d_key = rotary(d_kv[:, :HD], cos_q, -sin_q)
    d_key_raw, grad_key_gain = norm_back(key_raw[WINDOW:], r_k[WINDOW:], knorm_gain, d_key)
    d_key_raw = d_key_raw.astype(bf16)
    d_value = d_kv[:, HD:].astype(bf16)
    d_here = jnp.where(c == 0, d_key_raw, d_value)
    d_there = jnp.where(c == 0, d_value, d_key_raw)
    d_xn = (
        dot_nt(d_q_own, part_a[:, :512])
        + dot_nt(d_q_other, part_ao)
        + dot_nt(d_here, part_b[:, :HD])
        + dot_nt(d_there, part_bo[:, :HD])
    )
    d_x, grad_pre = norm_back(x, r_keys[WINDOW:], pre_gain, d_xn)
    d_tokens = (d_mid + d_x).astype(bf16)

    finished = [out_rows, dot_nt(d_tokens, order).astype(bf16)]
    finished = in_order(gather_rows(jnp.concatenate(finished, axis=1)), xh, c)
    output, grad_tokens = finished[:, :D], finished[:, D:]

    short_grads = dot_nt(jnp.stack([grad_query_gain, grad_key_gain]).astype(bf16), short_order)
    gain_grads = jnp.concatenate(
        [jnp.stack([grad_pre, grad_post, grad_ffn_pre, grad_ffn_post]), short_grads]
    )
    gain_grads = jnp.pad(gain_grads, ((0, 2), (0, 0))).T.astype(bf16)
    gain_grads = jnp.pad(gain_grads, ((0, 0), (0, 120)))
    own_a, own_b, other_a, other_b = attention_weights(
        xn,
        d_branch,
        gain_grads,
        (d_q_own, d_here, att[:, :512]),
        (d_q_other, d_there, att[:, 512:]),
    )
    sum_a = add(own_a, fetch(other_a, c=1)).astype(bf16)
    sum_b = add(own_b, fetch(other_b, c=1)).astype(bf16)
    sum_a, sum_b, ffn_sides = lax.optimization_barrier((sum_a, sum_b, ffn_sides))
    line_a, line_b = add(g_a[0], *ffn_sides[0]).astype(bf16), add(g_b[0], *ffn_sides[1]).astype(bf16)
    g_ffn = jnp.stack(
        [
            scatter_small([line_a[k] for k in range(4)], "z"),
            scatter_small([line_b[k] for k in range(4)], "y"),
        ]
    )
    sum_a, sum_b = blocks_of([sum_a], 0), blocks_of([sum_b], 1)
    halves = halves_out(sum_a, "y"), halves_out(sum_b, "z")
    halves = lax.optimization_barrier(halves)
    sides = sides_out(sum_a, halves[0], "y"), sides_out(sum_b, halves[1], "z")
    sides = lax.optimization_barrier(sides)
    line_a, line_b = add(sum_a[0], *sides[0]).astype(bf16), add(sum_b[0], *sides[1]).astype(bf16)
    sum_a = scatter_small([line_a[k] for k in range(4)], "z").astype(bf16)
    sum_b = scatter_small([line_b[k] for k in range(4)], "y").astype(bf16)

    g_ffn = add(g_ffn[:, :36], fetch(g_ffn[:, 36:].astype(bf16), xl=1))
    g_ffn = [
        jnp.concatenate([g_ffn[0, :, at : at + CUT], g_ffn[1, :, at : at + units - CUT]], axis=1)
        for at in (0, CUT, 2 * CUT)
    ]
    def parcel_back(xr_, xhr):
        a, b = sum_a[36 * xr_ : 36 * xr_ + 36], sum_b[36 * xr_ : 36 * xr_ + 36]
        kv = jnp.where(xh ^ xhr == 0, b[:18, :HD], b[18:, :HD]).reshape(36, 128)
        return jnp.concatenate(
            [a[:, 256 * xhr : 256 * xhr + 256], a[:, 512:], b[:, 256 + 256 * xhr : 512 + 256 * xhr], kv],
            axis=1,
        )

    total = add(
        parcel_back(0, 0),
        fetch(parcel_back(0, 1), xh=1),
        fetch(parcel_back(1, 0), xl=1),
        fetch(parcel_back(1, 1), xl=1, xh=1),
    )
    g_kv = total[:, 640:].reshape(18, 256)
    g_kv_here = jnp.where(c == 0, g_kv[:9], g_kv[9:])
    g_kv_away = fetch(jnp.where(c == 0, g_kv[9:], g_kv[:9]).astype(bf16), c=1).astype(f32)
    g_keyval = jnp.where(
        c == 0,
        jnp.concatenate([g_kv_here, g_kv_away], axis=1),
        jnp.concatenate([g_kv_away, g_kv_here], axis=1),
    )
    g_gains = total[:, 256:264].T
    return (
        output,
        grad_tokens,
        g_gains[0],
        total[:, :256],
        g_gains[4, :8],
        g_gains[5, :8],
        g_keyval,
        total[:, 384:640].T,
        g_gains[1],
        g_gains[2],
        g_ffn[0],
        g_ffn[1],
        g_ffn[2].T,
        g_gains[3],
    )


def solution(mesh):
    row, vector, weight, weight_t = P("seq", None), P("seq"), P("seq", "mp"), P("mp", "seq")
    keyval = P(("seq", "mp"), None)
    return jax.shard_map(
        per_device,
        mesh=mesh,
        in_specs=(row, row, vector, weight, vector, vector, keyval, weight_t)
        + (vector, vector, weight, weight, weight_t, vector),
        out_specs=(row, row, vector, weight, vector, vector, keyval, weight_t)
        + (vector, vector, weight, weight, weight_t, vector),
        check_vma=False,
    )
```

```python
import jax
import jax.numpy as jnp
from jax import lax
from jax.experimental import pallas as pl
from jax.experimental.pallas import tpu as pltpu
from jax.sharding import PartitionSpec as P

D = 1152
HD = 256
WINDOW = 512
SEQ_BLOCKS = 8
ROWS = 128
KEYS = ROWS + WINDOW
EPS = 1e-06
SCALE = 0.0625
MASKED = -1e30
SIZES = {"xl": 2, "z": 4, "y": 4, "xh": 2, "c": 2}
CUT = 896

bf16 = jnp.bfloat16
f32 = jnp.float32


def coords(n):
    mp, s = n % 4, n // 4
    return {"xl": s // 16, "z": s // 4 % 4, "y": s % 4, "xh": mp // 2, "c": mp % 2}


def flat(at):
    return ((at["xl"] * 4 + at["z"]) * 4 + at["y"]) * 4 + at["xh"] * 2 + at["c"]


def fetch(x, **delta):
    pairs = []
    for n in range(128):
        at = coords(n)
        for axis, by in delta.items():
            at[axis] = (at[axis] + by) % SIZES[axis]
        pairs.append((flat(at), n))
    return lax.ppermute(x, ("seq", "mp"), pairs)


def fetch_line(x, by):
    pairs = [(n + by, n) for n in range(128) if 0 <= n + by < 128]
    return lax.ppermute(x, ("seq", "mp"), pairs)


def gather_small(x, axis):
    return [x] + [fetch(x, **{axis: k}) for k in (1, 2, 3)]


def gather_big(x, axis):
    one = fetch(x, **{axis: 1})
    three = fetch(x, **{axis: 3})
    two = [fetch(one[:2], **{axis: 1}), fetch(three[2:], **{axis: 3})]
    return [x, one, jnp.concatenate(two, axis=0), three]


def gather_onward(x, axis):
    one = fetch(x, **{axis: 1})
    return [x, one, fetch(one, **{axis: 1}), fetch(x, **{axis: 3})]


def gather_grids(a, b, first):
    line_a, line_b = lax.optimization_barrier((first(a, "z"), first(b, "y")))
    grid_a = jnp.stack(gather_big(jnp.stack(line_a), "y"), axis=1)
    grid_b = jnp.stack(gather_big(jnp.stack(line_b), "z"), axis=0)
    return grid_a.reshape(D, a.shape[-1]), grid_b.reshape(D, b.shape[-1])


def add(*terms):
    total = terms[0].astype(f32)
    for term in terms[1:]:
        total = total + term.astype(f32)
    return total


def scatter_small(blocks, axis):
    return add(blocks[0], *[fetch(blocks[k], **{axis: 4 - k}) for k in (1, 2, 3)])


def blocks_of(parts, route):
    grids = [part.reshape(4, 4, 72, part.shape[-1]) for part in parts]
    return [
        jnp.concatenate([grid[:, k] if route == 0 else grid[k] for grid in grids], axis=-1)
        for k in range(4)
    ]


def halves_out(blocks, axis):
    return fetch(blocks[2][:2], **{axis: 3}), fetch(blocks[2][2:], **{axis: 1})


def sides_out(blocks, halves, axis):
    one = jnp.concatenate([add(blocks[1][:2], halves[0]).astype(bf16), blocks[1][2:]], axis=0)
    three = jnp.concatenate([blocks[3][:2], add(blocks[3][2:], halves[1]).astype(bf16)], axis=0)
    return fetch(one, **{axis: 3}), fetch(three, **{axis: 1})


def gather_rows(x):
    core = fetch(x, c=1)
    far = fetch(x, xh=1)
    return jnp.concatenate([x, core, far, fetch(far, c=1)], axis=0)


def scatter_rows(x):
    got = [fetch(x[ROWS : 2 * ROWS], c=1), fetch(x[3 * ROWS :], c=1)]
    far = add(x[2 * ROWS : 3 * ROWS], got[1]).astype(bf16)
    return add(x[:ROWS], got[0], fetch(far, xh=1))


def in_order(rows, xh, c):
    grid = rows.reshape(2, 2, ROWS, rows.shape[-1])
    grid = jnp.where(xh == 0, grid, grid[::-1])
    return jnp.where(c == 0, grid, grid[:, ::-1]).reshape(rows.shape)


def dot(a, b):
    return jnp.dot(a, b, preferred_element_type=f32)


def dot_nt(a, b):
    return lax.dot_general(a, b, (((1,), (1,)), ((), ())), preferred_element_type=f32)


def dot_tn(a, b):
    return lax.dot_general(a, b, (((0,), (0,)), ((), ())), preferred_element_type=f32)


def inverse_rms(v):
    return lax.rsqrt(jnp.mean(v * v, axis=-1, keepdims=True) + EPS)


def norm_back(v, r, g, e):
    ev = e * v
    inner = jnp.mean(g * ev, axis=-1, keepdims=True)
    gain_axes = tuple(range(v.ndim - 1))
    return r * (g * e) - v * (r * r * r * inner), jnp.sum(ev * r, axis=gain_axes)


def rotary(v, cosine, sine):
    former, latter = v[..., :128], v[..., 128:]
    return jnp.concatenate([former * cosine - latter * sine, latter * cosine + former * sine], axis=-1)


def gelu_tanh(v):
    return 0.5 * v * (1.0 + jnp.tanh(0.7978845608028654 * (v + 0.044715 * v * v * v)))


def gated_hidden(gate_in, up_in):
    return gelu_tanh(gate_in) * up_in


def in_vmem(count):
    return [pl.BlockSpec(memory_space=pltpu.VMEM)] * count


def forward_kernel(hn_ref, w_ref, prior_ref, gate_ref, up_ref, sum_ref):
    hn = hn_ref[...]
    gate = dot(hn, w_ref[:, :CUT])
    up = dot(hn, w_ref[:, CUT : 2 * CUT])
    hidden = gated_hidden(gate, up).astype(bf16)
    gate_ref[...] = gate.astype(bf16)
    up_ref[...] = up.astype(bf16)
    total = dot_nt(hidden, w_ref[:, 2 * CUT :])
    if prior_ref is not None:
        total = total + prior_ref[...]
    sum_ref[...] = total.astype(sum_ref.dtype)


def ffn_forward(hn, w, prior):
    first = prior is None
    rows = hn.shape[0]
    kernel = (lambda a, b, *out: forward_kernel(a, b, None, *out)) if first else forward_kernel
    args = (hn, w) if first else (hn, w, prior)
    return pl.pallas_call(
        kernel,
        out_shape=(
            jax.ShapeDtypeStruct((rows, CUT), bf16),
            jax.ShapeDtypeStruct((rows, CUT), bf16),
            jax.ShapeDtypeStruct((rows, D), f32 if first else bf16),
        ),
        in_specs=in_vmem(len(args)),
        out_specs=tuple(in_vmem(3)),
        compiler_params=pltpu.CompilerParams(vmem_limit_bytes=36 * 2**20),
        cost_estimate=pl.CostEstimate(
            flops=6 * rows * D * CUT, bytes_accessed=12 * 2**20, transcendentals=rows * CUT
        ),
    )(*args)


def backward_kernel(d_ffn_ref, w_ref, gate_ref, up_ref, prior_ref, grads_ref, sum_ref):
    d_hidden = dot(d_ffn_ref[...], w_ref[:, 2 * CUT :])
    gate, up = gate_ref[...].astype(f32), up_ref[...].astype(f32)
    square = gate * gate
    tanh = jnp.tanh(0.7978845608028654 * (gate + 0.044715 * square * gate))
    half = 0.5 * (1.0 + tanh)
    gelu = gate * half
    slope = half + 0.5 * gate * (1.0 - tanh * tanh) * (
        0.7978845608028654 * (1.0 + 3 * 0.044715 * square)
    )
    d_gate = (d_hidden * up * slope).astype(bf16)
    d_up = (d_hidden * gelu).astype(bf16)
    grads_ref[0] = d_gate
    grads_ref[1] = d_up
    grads_ref[2] = (gelu * up).astype(bf16)
    total = dot_nt(d_gate, w_ref[:, :CUT]) + dot_nt(d_up, w_ref[:, CUT : 2 * CUT])
    if prior_ref is not None:
        total = total + prior_ref[...]
    sum_ref[...] = total.astype(sum_ref.dtype)


def ffn_backward(d_ffn, w, gate, up, prior):
    first = prior is None
    rows = d_ffn.shape[0]
    kernel = (
        (lambda a, b, g, u, *out: backward_kernel(a, b, g, u, None, *out)) if first else backward_kernel
    )
    args = (d_ffn, w, gate, up) if first else (d_ffn, w, gate, up, prior)
    return pl.pallas_call(
        kernel,
        out_shape=(
            jax.ShapeDtypeStruct((3, rows, CUT), bf16),
            jax.ShapeDtypeStruct((rows, D), f32 if first else bf16),
        ),
        in_specs=in_vmem(len(args)),
        out_specs=tuple(in_vmem(2)),
        compiler_params=pltpu.CompilerParams(vmem_limit_bytes=36 * 2**20),
        cost_estimate=pl.CostEstimate(
            flops=6 * rows * D * CUT, bytes_accessed=14 * 2**20, transcendentals=rows * CUT
        ),
    )(*args)


def weights_kernel(route, hn_ref, d_ffn_ref, grads_ref, out_ref):
    def product(left_ref):
        total = dot_tn(left_ref[...], grads_ref[0]).astype(bf16)
        for zr in range(4):
            for yr in range(4):
                block = total[72 * (4 * zr + yr) : 72 * (4 * zr + yr) + 72]
                if route == 0:
                    out_ref[yr, zr] = block
                else:
                    out_ref[zr, yr] = block

    which = pl.program_id(0)

    @pl.when(which < 2)
    def _():
        product(hn_ref)

    @pl.when(which == 2)
    def _():
        product(d_ffn_ref)


def ffn_weights(hn, d_ffn, grads, route):
    rows = hn.shape[0]
    whole = pl.BlockSpec((rows, D), lambda j: (0, 0))
    return pl.pallas_call(
        lambda *refs: weights_kernel(route, *refs),
        grid=(3,),
        out_shape=jax.ShapeDtypeStruct((4, 4, 72, 3 * CUT), bf16),
        in_specs=[whole, whole, pl.BlockSpec((1, rows, CUT), lambda j: (j, 0, 0))],
        out_specs=pl.BlockSpec((4, 4, 72, CUT), lambda j: (0, 0, 0, j)),
        compiler_params=pltpu.CompilerParams(vmem_limit_bytes=36 * 2**20),
        cost_estimate=pl.CostEstimate(
            flops=6 * rows * D * CUT, bytes_accessed=12 * 2**20, transcendentals=0
        ),
    )(hn, d_ffn, grads)


def attention_weights_kernel(xn, d_branch, gains, *refs):
    sides, outs = refs[:6], refs[6:]
    for k in range(2):
        d_q, d_kv, att = sides[3 * k : 3 * k + 3]
        out_a, out_b = outs[2 * k : 2 * k + 2]
        out_a[:, :512] = dot_tn(xn[...], d_q[...]).astype(bf16)
        out_a[:, 512:] = gains[...]
        out_b[:, :HD] = dot_tn(xn[...], d_kv[...]).astype(bf16)
        out_b[:, HD:] = dot_tn(d_branch[...], att[...]).astype(bf16)


def attention_weights(xn, d_branch, gains, here, there):
    shapes = tuple(jax.ShapeDtypeStruct((D, n), bf16) for n in (640, 768, 640, 768))
    return pl.pallas_call(
        attention_weights_kernel,
        out_shape=shapes,
        in_specs=in_vmem(9),
        out_specs=tuple(in_vmem(4)),
        compiler_params=pltpu.CompilerParams(vmem_limit_bytes=24 * 2**20),
        cost_estimate=pl.CostEstimate(
            flops=2 * ROWS * D * 2560, bytes_accessed=8 * 2**20, transcendentals=0
        ),
    )(xn, d_branch, gains, *here, *there)


def per_device(
    tokens,
    grad_out,
    attn_pre_gain,
    w_query,
    query_gain,
    key_gain,
    w_keyval,
    w_out,
    attn_post_gain,
    ffn_pre_gain,
    w_gate,
    w_up,
    w_down,
    ffn_post_gain,
):
    seq = lax.axis_index("seq")
    mp = lax.axis_index("mp")
    xl, z, y = seq // 16, seq // 4 % 4, seq % 4
    xh, c = mp // 2, mp % 2

    kv_mine = lax.dynamic_slice_in_dim(w_keyval, 256 * c, 256, 1)
    kv_other = fetch(lax.dynamic_slice_in_dim(w_keyval, 256 * (1 - c), 256, 1), c=1)
    kv18 = jnp.where(
        c == 0,
        jnp.concatenate([kv_mine, kv_other], axis=0),
        jnp.concatenate([kv_other, kv_mine], axis=0),
    )
    short = jnp.pad(jnp.stack([query_gain, key_gain], axis=1), ((0, 28), (0, 0)))
    gains = jnp.stack([attn_pre_gain, attn_post_gain, ffn_pre_gain, ffn_post_gain], axis=1)
    gains = jnp.pad(jnp.concatenate([gains, short], axis=1), ((0, 0), (0, 122)))
    parcel = jnp.concatenate([w_query, gains, w_out.T, kv18.reshape(36, 128)], axis=1)
    half = fetch_line(lax.dynamic_slice_in_dim(tokens, 256 * c, 256, 0), -4)
    parcels = [
        [parcel, fetch(parcel, xh=1)],
        [fetch(parcel, xl=1), fetch(parcel, xl=1, xh=1)],
    ]
    parcels, half = lax.optimization_barrier((parcels, half))

    def kv36(pair):
        own, far = pair[0][:, 640:].reshape(18, 256), pair[1][:, 640:].reshape(18, 256)
        return jnp.where(
            xh == 0, jnp.concatenate([own, far], axis=0), jnp.concatenate([far, own], axis=0)
        )

    block_a = jnp.concatenate(
        [jnp.concatenate([p[0][:, :256], p[1][:, :256], p[0][:, 256:384]], axis=1) for p in parcels],
        axis=0,
    )
    block_b = jnp.concatenate(
        [jnp.concatenate([kv36(p), p[0][:, 384:640], p[1][:, 384:640]], axis=1) for p in parcels],
        axis=0,
    )
    part_a, part_b = gather_grids(block_a, block_b, gather_small)
    part_ao = fetch(part_a[:, :512], c=1)
    part_bo = fetch(part_b, c=1)

    units = w_down.shape[0]
    ffn_own = jnp.stack([w_gate, w_up, w_down.T])
    ffn_own = jnp.pad(ffn_own, ((0, 0), (0, 0), (0, 2 * CUT - units)))
    ffn_own = jnp.stack(
        [
            jnp.concatenate([ffn_own[k, :, half * CUT : half * CUT + CUT] for k in range(3)], axis=1)
            for half in range(2)
        ]
    )
    ffn_own, block_a = lax.optimization_barrier((ffn_own, block_a))
    ffn_pair = jnp.concatenate([ffn_own, fetch(ffn_own, xl=1)], axis=1)
    ffn_pair, part_a, part_b = lax.optimization_barrier((ffn_pair, part_a, part_b))
    part_fa, part_fb = gather_grids(ffn_pair[0], ffn_pair[1], gather_onward)

    half_other = fetch(half, c=1)
    before = jnp.where(
        c == 0,
        jnp.concatenate([half, half_other], axis=0),
        jnp.concatenate([half_other, half], axis=0),
    )
    rows = lax.dynamic_slice_in_dim(jnp.concatenate([before, tokens], axis=0), ROWS * mp, KEYS, 0)
    column = jnp.arange(D, dtype=jnp.int32)
    zr, yr, xr, place = column // 288, column // 72 % 4, column // 36 % 2, column % 36
    owner = (xl ^ xr) * 16 + (z + zr) % 4 * 4 + (y + yr) % 4
    order = (column[:, None] == (owner * 36 + place)[None, :]).astype(bf16)
    short_owner = jnp.where(place < 8, owner * 8 + place, -1)
    short_order = (short_owner[:, None] == jnp.arange(HD, dtype=jnp.int32)[None, :]).astype(bf16)
    x_keys = dot(rows, order).astype(bf16).astype(f32)
    x = x_keys[WINDOW:]
    e_out = dot(lax.dynamic_slice_in_dim(grad_out, ROWS * mp, ROWS, 0), order).astype(bf16).astype(f32)
    r_keys = inverse_rms(x_keys)

    gain_cols = part_a[:, 512:]
    gain_rows = gain_cols[:, :8].T.astype(f32)
    pre_gain, post_gain, ffn_pre, ffn_post = (gain_rows[k : k + 1] for k in range(4))
    short_rows = dot_tn(gain_cols, short_order)
    qnorm_gain, knorm_gain = short_rows[4:5], short_rows[5:6]

    first_pos = seq % SEQ_BLOCKS * 512 + ROWS * mp
    positions = (first_pos - WINDOW + jnp.arange(KEYS, dtype=jnp.int32)).astype(f32)
    exponent = jnp.arange(HD // 2, dtype=f32) * (-2.0 / HD)
    angle = positions[:, None] * jnp.power(10000.0, exponent)[None, :]
    cosine, sine = jnp.cos(angle), jnp.sin(angle)
    cos_q, sin_q = cosine[WINDOW:], sine[WINDOW:]
    xn_keys = (x_keys * r_keys * pre_gain).astype(bf16)
    xn = xn_keys[WINDOW:]
    q_raw = [dot(xn, part_a[:, :512]), dot(xn, part_ao)]
    q_raw = jnp.stack([q_raw[h // 2][:, h % 2 * HD : h % 2 * HD + HD] for h in range(4)])
    kv_here, kv_there = dot(xn_keys, part_b[:, :HD]), dot(xn_keys, part_bo[:, :HD])
    key_raw = jnp.where(c == 0, kv_here, kv_there)
    values = jnp.where(c == 0, kv_there, kv_here).astype(bf16)
    r_q, r_k = inverse_rms(q_raw), inverse_rms(key_raw)
    query = rotary(q_raw * r_q * qnorm_gain, cos_q, sin_q).astype(bf16).reshape(4 * ROWS, HD)
    keys = rotary(key_raw * r_k * knorm_gain, cosine, sine).astype(bf16)
    row_ids = jnp.arange(ROWS, dtype=jnp.int32)[:, None]
    key_ids = jnp.arange(KEYS, dtype=jnp.int32)[None, :]
    allowed = (key_ids > row_ids) & (key_ids <= row_ids + WINDOW) & (key_ids + first_pos >= WINDOW)
    score = dot_nt(query, keys).reshape(4, ROWS, KEYS) * SCALE
    score = jnp.where(allowed[None], score, MASKED)
    peak = jnp.max(score, axis=-1, keepdims=True)
    weight = jnp.exp(score - peak)
    prob = weight / jnp.sum(weight, axis=-1, keepdims=True)
    prob_low = prob.astype(bf16).reshape(4 * ROWS, KEYS)
    att = dot(prob_low, values).astype(bf16).reshape(4, ROWS, HD)
    att = jnp.concatenate([att[h] for h in range(4)], axis=1)
    out_own, out_other = part_b[:, HD:], part_bo[:, HD:]
    branch = dot_nt(att[:, :512], out_own) + dot_nt(att[:, 512:], out_other)
    r_branch = inverse_rms(branch)
    mid = x + branch * r_branch * post_gain
    r_mid = inverse_rms(mid)
    hn_rows = (mid * r_mid * ffn_pre).astype(bf16)

    hn = gather_rows(hn_rows)
    gate_a, up_a, partial = ffn_forward(hn, part_fa, None)
    gate_b, up_b, partial = ffn_forward(hn, part_fb, partial)
    ffn = scatter_rows(partial)
    r_ffn = inverse_rms(ffn)
    output_rows = (mid + ffn * r_ffn * ffn_post).astype(bf16)
    d_ffn_rows, grad_ffn_post = norm_back(ffn, r_ffn, ffn_post, e_out)
    d_ffn = gather_rows(d_ffn_rows.astype(bf16))
    grads_a, partial = ffn_backward(d_ffn, part_fa, gate_a, up_a, None)
    grads_b, partial = ffn_backward(d_ffn, part_fb, gate_b, up_b, partial)
    d_hn = scatter_rows(partial)
    g_a, g_b = ffn_weights(hn, d_ffn, grads_a, 0), ffn_weights(hn, d_ffn, grads_b, 1)
    halves = halves_out(g_a, "y"), halves_out(g_b, "z")

    d_mid, grad_ffn_pre = norm_back(mid, r_mid, ffn_pre, d_hn)
    d_mid = d_mid + e_out
    d_branch, grad_post = norm_back(branch, r_branch, post_gain, d_mid)
    d_branch = d_branch.astype(bf16)
    d_att = [dot(d_branch, out_own), dot(d_branch, out_other)]
    d_att = jnp.stack([d_att[h // 2][:, h % 2 * HD : h % 2 * HD + HD] for h in range(4)])
    d_att = d_att.astype(bf16).reshape(4 * ROWS, HD)
    d_att, halves, output_rows = lax.optimization_barrier((d_att, halves, output_rows))
    ffn_sides = sides_out(g_a, halves[0], "y"), sides_out(g_b, halves[1], "z")
    d_prob = dot_nt(d_att, values).reshape(4, ROWS, KEYS)
    delta = jnp.sum(prob * d_prob, axis=-1, keepdims=True)
    d_score = (prob * (d_prob - delta)).astype(bf16).reshape(4 * ROWS, KEYS)
    d_query = dot(d_score, keys).reshape(4, ROWS, HD) * SCALE
    d_kv = jnp.concatenate(
        [dot_tn(d_score, query) * SCALE, dot_tn(prob_low, d_att)], axis=1
    ).reshape(5, ROWS, 2 * HD)
    d_kv_low = d_kv[:4].astype(bf16)
    d_q_raw, grad_query_gain = norm_back(q_raw, r_q, qnorm_gain, rotary(d_query, cos_q, -sin_q))
    d_q_raw = d_q_raw.astype(bf16)
    d_q_own = jnp.concatenate([d_q_raw[0], d_q_raw[1]], axis=1)
    d_q_other = jnp.concatenate([d_q_raw[2], d_q_raw[3]], axis=1)
    d_kv_away = []
    for k in range(4):
        part = d_kv_low[k]
        if k:
            part, d_kv_away[-1] = lax.optimization_barrier((part, d_kv_away[-1]))
        d_kv_away.append(fetch_line(part, 4 - k))
    d_kv = add(d_kv[4], *d_kv_away)
    d_key = rotary(d_kv[:, :HD], cos_q, -sin_q)
    d_key_raw, grad_key_gain = norm_back(key_raw[WINDOW:], r_k[WINDOW:], knorm_gain, d_key)
    d_key_raw = d_key_raw.astype(bf16)
    d_value = d_kv[:, HD:].astype(bf16)
    d_here = jnp.where(c == 0, d_key_raw, d_value)
    d_there = jnp.where(c == 0, d_value, d_key_raw)
    d_xn = (
        dot_nt(d_q_own, part_a[:, :512])
        + dot_nt(d_q_other, part_ao)
        + dot_nt(d_here, part_b[:, :HD])
        + dot_nt(d_there, part_bo[:, :HD])
    )
    d_x, grad_pre = norm_back(x, r_keys[WINDOW:], pre_gain, d_xn)
    d_tokens = (d_mid + d_x).astype(bf16)

    short_grads = dot_nt(jnp.stack([grad_query_gain, grad_key_gain]).astype(bf16), short_order)
    gain_grads = jnp.concatenate(
        [jnp.stack([grad_pre, grad_post, grad_ffn_pre, grad_ffn_post]), short_grads]
    )
    gain_grads = jnp.pad(gain_grads, ((0, 2), (0, 0))).T.astype(bf16)
    gain_grads = jnp.pad(gain_grads, ((0, 0), (0, 120)))
    own_a, own_b, other_a, other_b = attention_weights(
        xn,
        d_branch,
        gain_grads,
        (d_q_own, d_here, att[:, :512]),
        (d_q_other, d_there, att[:, 512:]),
    )
    finished = [dot_nt(v, order).astype(bf16) for v in (output_rows, d_tokens)]
    own_a, own_b, other_a, other_b, ffn_sides, finished = lax.optimization_barrier(
        (own_a, own_b, other_a, other_b, ffn_sides, finished)
    )
    sum_a = add(own_a, fetch(other_a, c=1)).astype(bf16)
    sum_b = add(own_b, fetch(other_b, c=1)).astype(bf16)
    line_a, line_b = add(g_a[0], *ffn_sides[0]).astype(bf16), add(g_b[0], *ffn_sides[1]).astype(bf16)
    sum_a, sum_b, line_a, line_b = lax.optimization_barrier((sum_a, sum_b, line_a, line_b))
    g_ffn = jnp.stack(
        [
            scatter_small([line_a[k] for k in range(4)], "z"),
            scatter_small([line_b[k] for k in range(4)], "y"),
        ]
    )
    sum_a, sum_b = blocks_of([sum_a], 0), blocks_of([sum_b], 1)
    halves = halves_out(sum_a, "y"), halves_out(sum_b, "z")
    halves, finished = lax.optimization_barrier((halves, finished))
    sides = sides_out(sum_a, halves[0], "y"), sides_out(sum_b, halves[1], "z")
    sides = lax.optimization_barrier(sides)
    line_a, line_b = add(sum_a[0], *sides[0]).astype(bf16), add(sum_b[0], *sides[1]).astype(bf16)
    sum_a = scatter_small([line_a[k] for k in range(4)], "z").astype(bf16)
    sum_b = scatter_small([line_b[k] for k in range(4)], "y").astype(bf16)

    g_ffn = add(g_ffn[:, :36], fetch(g_ffn[:, 36:].astype(bf16), xl=1))
    g_ffn = [
        jnp.concatenate([g_ffn[0, :, at : at + CUT], g_ffn[1, :, at : at + units - CUT]], axis=1)
        for at in (0, CUT, 2 * CUT)
    ]
    finished = in_order(gather_rows(jnp.concatenate(finished, axis=1)), xh, c)
    output, grad_tokens = finished[:, :D], finished[:, D:]

    def parcel_back(xr_, xhr):
        a, b = sum_a[36 * xr_ : 36 * xr_ + 36], sum_b[36 * xr_ : 36 * xr_ + 36]
        kv = jnp.where(xh ^ xhr == 0, b[:18, :HD], b[18:, :HD]).reshape(36, 128)
        return jnp.concatenate(
            [a[:, 256 * xhr : 256 * xhr + 256], a[:, 512:], b[:, 256 + 256 * xhr : 512 + 256 * xhr], kv],
            axis=1,
        )

    total = add(
        parcel_back(0, 0),
        fetch(parcel_back(0, 1), xh=1),
        fetch(parcel_back(1, 0), xl=1),
        fetch(parcel_back(1, 1), xl=1, xh=1),
    )
    g_kv = total[:, 640:].reshape(18, 256)
    g_kv_here = jnp.where(c == 0, g_kv[:9], g_kv[9:])
    g_kv_away = fetch(jnp.where(c == 0, g_kv[9:], g_kv[:9]).astype(bf16), c=1).astype(f32)
    g_keyval = jnp.where(
        c == 0,
        jnp.concatenate([g_kv_here, g_kv_away], axis=1),
        jnp.concatenate([g_kv_away, g_kv_here], axis=1),
    )
    g_gains = total[:, 256:264].T
    return (
        output,
        grad_tokens,
        g_gains[0],
        total[:, :256],
        g_gains[4, :8],
        g_gains[5, :8],
        g_keyval,
        total[:, 384:640].T,
        g_gains[1],
        g_gains[2],
        g_ffn[0],
        g_ffn[1],
        g_ffn[2].T,
        g_gains[3],
    )


def solution(mesh):
    row, vector, weight, weight_t = P("seq", None), P("seq"), P("seq", "mp"), P("mp", "seq")
    keyval = P(("seq", "mp"), None)
    return jax.shard_map(
        per_device,
        mesh=mesh,
        in_specs=(row, row, vector, weight, vector, vector, keyval, weight_t)
        + (vector, vector, weight, weight, weight_t, vector),
        out_specs=(row, row, vector, weight, vector, vector, keyval, weight_t)
        + (vector, vector, weight, weight, weight_t, vector),
        check_vma=False,
    )
```

```python
import jax
import jax.numpy as jnp
from jax import lax
from jax.experimental import pallas as pl
from jax.experimental.pallas import tpu as pltpu
from jax.sharding import PartitionSpec as P

D = 1152
HD = 256
WINDOW = 512
SEQ_BLOCKS = 8
ROWS = 128
KEYS = ROWS + WINDOW
EPS = 1e-06
SCALE = 0.0625
MASKED = -1e30
SIZES = {"xl": 2, "z": 4, "y": 4, "xh": 2, "c": 2}
CUT = 896

bf16 = jnp.bfloat16
f32 = jnp.float32


def coords(n):
    mp, s = n % 4, n // 4
    return {"xl": s // 16, "z": s // 4 % 4, "y": s % 4, "xh": mp // 2, "c": mp % 2}


def flat(at):
    return ((at["xl"] * 4 + at["z"]) * 4 + at["y"]) * 4 + at["xh"] * 2 + at["c"]


def fetch(x, **delta):
    pairs = []
    for n in range(128):
        at = coords(n)
        for axis, by in delta.items():
            at[axis] = (at[axis] + by) % SIZES[axis]
        pairs.append((flat(at), n))
    return lax.ppermute(x, ("seq", "mp"), pairs)


def fetch_line(x, by):
    pairs = [(n + by, n) for n in range(128) if 0 <= n + by < 128]
    return lax.ppermute(x, ("seq", "mp"), pairs)


def gather_small(x, axis):
    return [x] + [fetch(x, **{axis: k}) for k in (1, 2, 3)]


def gather_big(x, axis):
    one = fetch(x, **{axis: 1})
    three = fetch(x, **{axis: 3})
    two = [fetch(one[:2], **{axis: 1}), fetch(three[2:], **{axis: 3})]
    return [x, one, jnp.concatenate(two, axis=0), three]


def gather_onward(x, axis):
    one = fetch(x, **{axis: 1})
    return [x, one, fetch(one, **{axis: 1}), fetch(x, **{axis: 3})]


def gather_grids(a, b, first):
    line_a, line_b = lax.optimization_barrier((first(a, "z"), first(b, "y")))
    grid_a = jnp.stack(gather_big(jnp.stack(line_a), "y"), axis=1)
    grid_b = jnp.stack(gather_big(jnp.stack(line_b), "z"), axis=0)
    return grid_a.reshape(D, a.shape[-1]), grid_b.reshape(D, b.shape[-1])


def add(*terms):
    total = terms[0].astype(f32)
    for term in terms[1:]:
        total = total + term.astype(f32)
    return total


def scatter_small(blocks, axis):
    return add(blocks[0], *[fetch(blocks[k], **{axis: 4 - k}) for k in (1, 2, 3)])


def blocks_of(parts, route):
    grids = [part.reshape(4, 4, 72, part.shape[-1]) for part in parts]
    return [
        jnp.concatenate([grid[:, k] if route == 0 else grid[k] for grid in grids], axis=-1)
        for k in range(4)
    ]


def halves_out(blocks, axis):
    return fetch(blocks[2][:2], **{axis: 3}), fetch(blocks[2][2:], **{axis: 1})


def sides_of(blocks, halves):
    one = jnp.concatenate([add(blocks[1][:2], halves[0]).astype(bf16), blocks[1][2:]], axis=0)
    three = jnp.concatenate([blocks[3][:2], add(blocks[3][2:], halves[1]).astype(bf16)], axis=0)
    return one, three


def sides_out(sides, axis):
    return fetch(sides[0], **{axis: 3}), fetch(sides[1], **{axis: 1})


def gather_rows(x):
    core = fetch(x, c=1)
    far = fetch(x, xh=1)
    return jnp.concatenate([x, core, far, fetch(far, c=1)], axis=0)


def scatter_rows(x):
    got = [fetch(x[ROWS : 2 * ROWS], c=1), fetch(x[3 * ROWS :], c=1)]
    far = add(x[2 * ROWS : 3 * ROWS], got[1]).astype(bf16)
    return add(x[:ROWS], got[0], fetch(far, xh=1))


def in_order(rows, xh, c):
    grid = rows.reshape(2, 2, ROWS, rows.shape[-1])
    grid = jnp.where(xh == 0, grid, grid[::-1])
    return jnp.where(c == 0, grid, grid[:, ::-1]).reshape(rows.shape)


def dot(a, b):
    return jnp.dot(a, b, preferred_element_type=f32)


def dot_nt(a, b):
    return lax.dot_general(a, b, (((1,), (1,)), ((), ())), preferred_element_type=f32)


def dot_tn(a, b):
    return lax.dot_general(a, b, (((0,), (0,)), ((), ())), preferred_element_type=f32)


def inverse_rms(v):
    return lax.rsqrt(jnp.mean(v * v, axis=-1, keepdims=True) + EPS)


def norm_back(v, r, g, e):
    ev = e * v
    inner = jnp.mean(g * ev, axis=-1, keepdims=True)
    gain_axes = tuple(range(v.ndim - 1))
    return r * (g * e) - v * (r * r * r * inner), jnp.sum(ev * r, axis=gain_axes)


def rotary(v, cosine, sine):
    former, latter = v[..., :128], v[..., 128:]
    return jnp.concatenate([former * cosine - latter * sine, latter * cosine + former * sine], axis=-1)


def gelu_tanh(v):
    return 0.5 * v * (1.0 + jnp.tanh(0.7978845608028654 * (v + 0.044715 * v * v * v)))


def gated_hidden(gate_in, up_in):
    return gelu_tanh(gate_in) * up_in


def in_vmem(count):
    return [pl.BlockSpec(memory_space=pltpu.VMEM)] * count


def forward_kernel(hn_ref, w_ref, prior_ref, gate_ref, up_ref, sum_ref):
    hn = hn_ref[...]
    gate = dot(hn, w_ref[:, :CUT])
    up = dot(hn, w_ref[:, CUT : 2 * CUT])
    hidden = gated_hidden(gate, up).astype(bf16)
    gate_ref[...] = gate.astype(bf16)
    up_ref[...] = up.astype(bf16)
    total = dot_nt(hidden, w_ref[:, 2 * CUT :])
    if prior_ref is not None:
        total = total + prior_ref[...]
    sum_ref[...] = total.astype(sum_ref.dtype)


def ffn_forward(hn, w, prior):
    first = prior is None
    rows = hn.shape[0]
    kernel = (lambda a, b, *out: forward_kernel(a, b, None, *out)) if first else forward_kernel
    args = (hn, w) if first else (hn, w, prior)
    return pl.pallas_call(
        kernel,
        out_shape=(
            jax.ShapeDtypeStruct((rows, CUT), bf16),
            jax.ShapeDtypeStruct((rows, CUT), bf16),
            jax.ShapeDtypeStruct((rows, D), f32 if first else bf16),
        ),
        in_specs=in_vmem(len(args)),
        out_specs=tuple(in_vmem(3)),
        compiler_params=pltpu.CompilerParams(vmem_limit_bytes=36 * 2**20),
        cost_estimate=pl.CostEstimate(
            flops=6 * rows * D * CUT, bytes_accessed=12 * 2**20, transcendentals=rows * CUT
        ),
    )(*args)


def backward_kernel(d_ffn_ref, w_ref, gate_ref, up_ref, prior_ref, grads_ref, sum_ref):
    d_hidden = dot(d_ffn_ref[...], w_ref[:, 2 * CUT :])
    gate, up = gate_ref[...].astype(f32), up_ref[...].astype(f32)
    square = gate * gate
    tanh = jnp.tanh(0.7978845608028654 * (gate + 0.044715 * square * gate))
    half = 0.5 * (1.0 + tanh)
    gelu = gate * half
    slope = half + 0.5 * gate * (1.0 - tanh * tanh) * (
        0.7978845608028654 * (1.0 + 3 * 0.044715 * square)
    )
    d_gate = (d_hidden * up * slope).astype(bf16)
    d_up = (d_hidden * gelu).astype(bf16)
    grads_ref[0] = d_gate
    grads_ref[1] = d_up
    grads_ref[2] = (gelu * up).astype(bf16)
    total = dot_nt(d_gate, w_ref[:, :CUT]) + dot_nt(d_up, w_ref[:, CUT : 2 * CUT])
    if prior_ref is not None:
        total = total + prior_ref[...]
    sum_ref[...] = total.astype(sum_ref.dtype)


def ffn_backward(d_ffn, w, gate, up, prior):
    first = prior is None
    rows = d_ffn.shape[0]
    kernel = (
        (lambda a, b, g, u, *out: backward_kernel(a, b, g, u, None, *out)) if first else backward_kernel
    )
    args = (d_ffn, w, gate, up) if first else (d_ffn, w, gate, up, prior)
    return pl.pallas_call(
        kernel,
        out_shape=(
            jax.ShapeDtypeStruct((3, rows, CUT), bf16),
            jax.ShapeDtypeStruct((rows, D), f32 if first else bf16),
        ),
        in_specs=in_vmem(len(args)),
        out_specs=tuple(in_vmem(2)),
        compiler_params=pltpu.CompilerParams(vmem_limit_bytes=36 * 2**20),
        cost_estimate=pl.CostEstimate(
            flops=6 * rows * D * CUT, bytes_accessed=14 * 2**20, transcendentals=rows * CUT
        ),
    )(*args)


def weights_kernel(route, hn_ref, d_ffn_ref, grads_ref, out_ref):
    def product(left_ref):
        total = dot_tn(left_ref[...], grads_ref[0]).astype(bf16)
        for zr in range(4):
            for yr in range(4):
                block = total[72 * (4 * zr + yr) : 72 * (4 * zr + yr) + 72]
                if route == 0:
                    out_ref[yr, zr] = block
                else:
                    out_ref[zr, yr] = block

    which = pl.program_id(0)

    @pl.when(which < 2)
    def _():
        product(hn_ref)

    @pl.when(which == 2)
    def _():
        product(d_ffn_ref)


def ffn_weights(hn, d_ffn, grads, route):
    rows = hn.shape[0]
    whole = pl.BlockSpec((rows, D), lambda j: (0, 0))
    return pl.pallas_call(
        lambda *refs: weights_kernel(route, *refs),
        grid=(3,),
        out_shape=jax.ShapeDtypeStruct((4, 4, 72, 3 * CUT), bf16),
        in_specs=[whole, whole, pl.BlockSpec((1, rows, CUT), lambda j: (j, 0, 0))],
        out_specs=pl.BlockSpec((4, 4, 72, CUT), lambda j: (0, 0, 0, j)),
        compiler_params=pltpu.CompilerParams(vmem_limit_bytes=36 * 2**20),
        cost_estimate=pl.CostEstimate(
            flops=6 * rows * D * CUT, bytes_accessed=12 * 2**20, transcendentals=0
        ),
    )(hn, d_ffn, grads)


def attention_weights_kernel(xn, d_branch, gains, *refs):
    sides, outs = refs[:6], refs[6:]
    for k in range(2):
        d_q, d_kv, att = sides[3 * k : 3 * k + 3]
        out_a, out_b = outs[2 * k : 2 * k + 2]
        out_a[:, :512] = dot_tn(xn[...], d_q[...]).astype(bf16)
        out_a[:, 512:] = gains[...]
        out_b[:, :HD] = dot_tn(xn[...], d_kv[...]).astype(bf16)
        out_b[:, HD:] = dot_tn(d_branch[...], att[...]).astype(bf16)


def attention_weights(xn, d_branch, gains, here, there):
    shapes = tuple(jax.ShapeDtypeStruct((D, n), bf16) for n in (640, 768, 640, 768))
    return pl.pallas_call(
        attention_weights_kernel,
        out_shape=shapes,
        in_specs=in_vmem(9),
        out_specs=tuple(in_vmem(4)),
        compiler_params=pltpu.CompilerParams(vmem_limit_bytes=24 * 2**20),
        cost_estimate=pl.CostEstimate(
            flops=2 * ROWS * D * 2560, bytes_accessed=8 * 2**20, transcendentals=0
        ),
    )(xn, d_branch, gains, *here, *there)


def per_device(
    tokens,
    grad_out,
    attn_pre_gain,
    w_query,
    query_gain,
    key_gain,
    w_keyval,
    w_out,
    attn_post_gain,
    ffn_pre_gain,
    w_gate,
    w_up,
    w_down,
    ffn_post_gain,
):
    seq = lax.axis_index("seq")
    mp = lax.axis_index("mp")
    xl, z, y = seq // 16, seq // 4 % 4, seq % 4
    xh, c = mp // 2, mp % 2

    kv_mine = lax.dynamic_slice_in_dim(w_keyval, 256 * c, 256, 1)
    kv_other = fetch(lax.dynamic_slice_in_dim(w_keyval, 256 * (1 - c), 256, 1), c=1)
    kv18 = jnp.where(
        c == 0,
        jnp.concatenate([kv_mine, kv_other], axis=0),
        jnp.concatenate([kv_other, kv_mine], axis=0),
    )
    short = jnp.pad(jnp.stack([query_gain, key_gain], axis=1), ((0, 28), (0, 0)))
    gains = jnp.stack([attn_pre_gain, attn_post_gain, ffn_pre_gain, ffn_post_gain], axis=1)
    gains = jnp.pad(jnp.concatenate([gains, short], axis=1), ((0, 0), (0, 122)))
    parcel = jnp.concatenate([w_query, gains, w_out.T, kv18.reshape(36, 128)], axis=1)
    half = fetch_line(lax.dynamic_slice_in_dim(tokens, 256 * c, 256, 0), -4)
    parcels = [
        [parcel, fetch(parcel, xh=1)],
        [fetch(parcel, xl=1), fetch(parcel, xl=1, xh=1)],
    ]
    parcels, half = lax.optimization_barrier((parcels, half))

    def kv36(pair):
        own, far = pair[0][:, 640:].reshape(18, 256), pair[1][:, 640:].reshape(18, 256)
        return jnp.where(
            xh == 0, jnp.concatenate([own, far], axis=0), jnp.concatenate([far, own], axis=0)
        )

    block_a = jnp.concatenate(
        [jnp.concatenate([p[0][:, :256], p[1][:, :256], p[0][:, 256:384]], axis=1) for p in parcels],
        axis=0,
    )
    block_b = jnp.concatenate(
        [jnp.concatenate([kv36(p), p[0][:, 384:640], p[1][:, 384:640]], axis=1) for p in parcels],
        axis=0,
    )
    part_a, part_b = gather_grids(block_a, block_b, gather_small)
    part_ao = fetch(part_a[:, :512], c=1)
    part_bo = fetch(part_b, c=1)

    units = w_down.shape[0]
    ffn_own = jnp.stack([w_gate, w_up, w_down.T])
    ffn_own = jnp.pad(ffn_own, ((0, 0), (0, 0), (0, 2 * CUT - units)))
    ffn_own = jnp.stack(
        [
            jnp.concatenate([ffn_own[k, :, half * CUT : half * CUT + CUT] for k in range(3)], axis=1)
            for half in range(2)
        ]
    )
    ffn_own, block_a = lax.optimization_barrier((ffn_own, block_a))
    ffn_pair = jnp.concatenate([ffn_own, fetch(ffn_own, xl=1)], axis=1)
    ffn_pair, part_a, part_b = lax.optimization_barrier((ffn_pair, part_a, part_b))
    part_fa, part_fb = gather_grids(ffn_pair[0], ffn_pair[1], gather_onward)

    half_other = fetch(half, c=1)
    before = jnp.where(
        c == 0,
        jnp.concatenate([half, half_other], axis=0),
        jnp.concatenate([half_other, half], axis=0),
    )
    rows = lax.dynamic_slice_in_dim(jnp.concatenate([before, tokens], axis=0), ROWS * mp, KEYS, 0)
    column = jnp.arange(D, dtype=jnp.int32)
    zr, yr, xr, place = column // 288, column // 72 % 4, column // 36 % 2, column % 36
    owner = (xl ^ xr) * 16 + (z + zr) % 4 * 4 + (y + yr) % 4
    order = (column[:, None] == (owner * 36 + place)[None, :]).astype(bf16)
    short_owner = jnp.where(place < 8, owner * 8 + place, -1)
    short_order = (short_owner[:, None] == jnp.arange(HD, dtype=jnp.int32)[None, :]).astype(bf16)
    x_keys = dot(rows, order).astype(bf16).astype(f32)
    x = x_keys[WINDOW:]
    e_out = dot(lax.dynamic_slice_in_dim(grad_out, ROWS * mp, ROWS, 0), order).astype(bf16).astype(f32)
    r_keys = inverse_rms(x_keys)

    gain_cols = part_a[:, 512:]
    gain_rows = gain_cols[:, :8].T.astype(f32)
    pre_gain, post_gain, ffn_pre, ffn_post = (gain_rows[k : k + 1] for k in range(4))
    short_rows = dot_tn(gain_cols, short_order)
    qnorm_gain, knorm_gain = short_rows[4:5], short_rows[5:6]

    first_pos = seq % SEQ_BLOCKS * 512 + ROWS * mp
    positions = (first_pos - WINDOW + jnp.arange(KEYS, dtype=jnp.int32)).astype(f32)
    exponent = jnp.arange(HD // 2, dtype=f32) * (-2.0 / HD)
    angle = positions[:, None] * jnp.power(10000.0, exponent)[None, :]
    cosine, sine = jnp.cos(angle), jnp.sin(angle)
    cos_q, sin_q = cosine[WINDOW:], sine[WINDOW:]
    xn_keys = (x_keys * r_keys * pre_gain).astype(bf16)
    xn = xn_keys[WINDOW:]
    q_raw = [dot(xn, part_a[:, :512]), dot(xn, part_ao)]
    q_raw = jnp.stack([q_raw[h // 2][:, h % 2 * HD : h % 2 * HD + HD] for h in range(4)])
    kv_here, kv_there = dot(xn_keys, part_b[:, :HD]), dot(xn_keys, part_bo[:, :HD])
    key_raw = jnp.where(c == 0, kv_here, kv_there)
    values = jnp.where(c == 0, kv_there, kv_here).astype(bf16)
    r_q, r_k = inverse_rms(q_raw), inverse_rms(key_raw)
    query = rotary(q_raw * r_q * qnorm_gain, cos_q, sin_q).astype(bf16).reshape(4 * ROWS, HD)
    keys = rotary(key_raw * r_k * knorm_gain, cosine, sine).astype(bf16)
    row_ids = jnp.arange(ROWS, dtype=jnp.int32)[:, None]
    key_ids = jnp.arange(KEYS, dtype=jnp.int32)[None, :]
    allowed = (key_ids > row_ids) & (key_ids <= row_ids + WINDOW) & (key_ids + first_pos >= WINDOW)
    score = dot_nt(query, keys).reshape(4, ROWS, KEYS) * SCALE
    score = jnp.where(allowed[None], score, MASKED)
    peak = jnp.max(score, axis=-1, keepdims=True)
    weight = jnp.exp(score - peak)
    prob = weight / jnp.sum(weight, axis=-1, keepdims=True)
    prob_low = prob.astype(bf16).reshape(4 * ROWS, KEYS)
    att = dot(prob_low, values).astype(bf16).reshape(4, ROWS, HD)
    att = jnp.concatenate([att[h] for h in range(4)], axis=1)
    out_own, out_other = part_b[:, HD:], part_bo[:, HD:]
    branch = dot_nt(att[:, :512], out_own) + dot_nt(att[:, 512:], out_other)
    r_branch = inverse_rms(branch)
    mid = x + branch * r_branch * post_gain
    r_mid = inverse_rms(mid)
    hn_rows = (mid * r_mid * ffn_pre).astype(bf16)

    hn = gather_rows(hn_rows)
    gate_a, up_a, partial = ffn_forward(hn, part_fa, None)
    gate_b, up_b, partial = ffn_forward(hn, part_fb, partial)
    ffn = scatter_rows(partial)
    r_ffn = inverse_rms(ffn)
    output_rows = (mid + ffn * r_ffn * ffn_post).astype(bf16)
    d_ffn_rows, grad_ffn_post = norm_back(ffn, r_ffn, ffn_post, e_out)
    d_ffn = gather_rows(d_ffn_rows.astype(bf16))
    grads_a, partial = ffn_backward(d_ffn, part_fa, gate_a, up_a, None)
    grads_b, partial = ffn_backward(d_ffn, part_fb, gate_b, up_b, partial)
    d_hn = scatter_rows(partial)
    g_a, g_b = ffn_weights(hn, d_ffn, grads_a, 0), ffn_weights(hn, d_ffn, grads_b, 1)
    halves = halves_out(g_a, "y"), halves_out(g_b, "z")

    d_mid, grad_ffn_pre = norm_back(mid, r_mid, ffn_pre, d_hn)
    d_mid = d_mid + e_out
    d_branch, grad_post = norm_back(branch, r_branch, post_gain, d_mid)
    d_branch = d_branch.astype(bf16)
    d_att = [dot(d_branch, out_own), dot(d_branch, out_other)]
    d_att = jnp.stack([d_att[h // 2][:, h % 2 * HD : h % 2 * HD + HD] for h in range(4)])
    d_att = d_att.astype(bf16).reshape(4 * ROWS, HD)
    d_att, halves, output_rows = lax.optimization_barrier((d_att, halves, output_rows))
    ffn_sides = sides_of(g_a, halves[0]), sides_of(g_b, halves[1])
    d_prob = dot_nt(d_att, values).reshape(4, ROWS, KEYS)
    delta = jnp.sum(prob * d_prob, axis=-1, keepdims=True)
    d_score = (prob * (d_prob - delta)).astype(bf16).reshape(4 * ROWS, KEYS)
    d_query = dot(d_score, keys).reshape(4, ROWS, HD) * SCALE
    d_kv = jnp.concatenate(
        [dot_tn(d_score, query) * SCALE, dot_tn(prob_low, d_att)], axis=1
    ).reshape(5, ROWS, 2 * HD)
    d_kv_low = d_kv[:4].astype(bf16)
    d_q_raw, grad_query_gain = norm_back(q_raw, r_q, qnorm_gain, rotary(d_query, cos_q, -sin_q))
    d_q_raw = d_q_raw.astype(bf16)
    d_q_own = jnp.concatenate([d_q_raw[0], d_q_raw[1]], axis=1)
    d_q_other = jnp.concatenate([d_q_raw[2], d_q_raw[3]], axis=1)
    d_kv_low, ffn_sides = lax.optimization_barrier((d_kv_low, ffn_sides))
    d_kv_away = [fetch_line(d_kv_low[k], 4 - k) for k in range(4)]
    ffn_sides = sides_out(ffn_sides[0], "y"), sides_out(ffn_sides[1], "z")
    d_kv = add(d_kv[4], *d_kv_away)
    d_key = rotary(d_kv[:, :HD], cos_q, -sin_q)
    d_key_raw, grad_key_gain = norm_back(key_raw[WINDOW:], r_k[WINDOW:], knorm_gain, d_key)
    d_key_raw = d_key_raw.astype(bf16)
    d_value = d_kv[:, HD:].astype(bf16)
    d_here = jnp.where(c == 0, d_key_raw, d_value)
    d_there = jnp.where(c == 0, d_value, d_key_raw)
    d_xn = (
        dot_nt(d_q_own, part_a[:, :512])
        + dot_nt(d_q_other, part_ao)
        + dot_nt(d_here, part_b[:, :HD])
        + dot_nt(d_there, part_bo[:, :HD])
    )
    d_x, grad_pre = norm_back(x, r_keys[WINDOW:], pre_gain, d_xn)
    d_tokens = (d_mid + d_x).astype(bf16)

    short_grads = dot_nt(jnp.stack([grad_query_gain, grad_key_gain]).astype(bf16), short_order)
    gain_grads = jnp.concatenate(
        [jnp.stack([grad_pre, grad_post, grad_ffn_pre, grad_ffn_post]), short_grads]
    )
    gain_grads = jnp.pad(gain_grads, ((0, 2), (0, 0))).T.astype(bf16)
    gain_grads = jnp.pad(gain_grads, ((0, 0), (0, 120)))
    own_a, own_b, other_a, other_b = attention_weights(
        xn,
        d_branch,
        gain_grads,
        (d_q_own, d_here, att[:, :512]),
        (d_q_other, d_there, att[:, 512:]),
    )
    finished = [dot_nt(v, order).astype(bf16) for v in (output_rows, d_tokens)]
    own_a, own_b, other_a, other_b, ffn_sides, finished = lax.optimization_barrier(
        (own_a, own_b, other_a, other_b, ffn_sides, finished)
    )
    sum_a = add(own_a, fetch(other_a, c=1)).astype(bf16)
    sum_b = add(own_b, fetch(other_b, c=1)).astype(bf16)
    sum_a, sum_b, ffn_sides = lax.optimization_barrier((sum_a, sum_b, ffn_sides))
    line_a, line_b = add(g_a[0], *ffn_sides[0]).astype(bf16), add(g_b[0], *ffn_sides[1]).astype(bf16)
    g_ffn = jnp.stack(
        [
            scatter_small([line_a[k] for k in range(4)], "z"),
            scatter_small([line_b[k] for k in range(4)], "y"),
        ]
    )
    sum_a, sum_b = blocks_of([sum_a], 0), blocks_of([sum_b], 1)
    halves = halves_out(sum_a, "y"), halves_out(sum_b, "z")
    halves, finished = lax.optimization_barrier((halves, finished))
    sides = sides_of(sum_a, halves[0]), sides_of(sum_b, halves[1])
    sides = sides_out(sides[0], "y"), sides_out(sides[1], "z")
    sides = lax.optimization_barrier(sides)
    line_a, line_b = add(sum_a[0], *sides[0]).astype(bf16), add(sum_b[0], *sides[1]).astype(bf16)
    sum_a = scatter_small([line_a[k] for k in range(4)], "z").astype(bf16)
    sum_b = scatter_small([line_b[k] for k in range(4)], "y").astype(bf16)

    g_ffn = add(g_ffn[:, :36], fetch(g_ffn[:, 36:].astype(bf16), xl=1))
    g_ffn = [
        jnp.concatenate([g_ffn[0, :, at : at + CUT], g_ffn[1, :, at : at + units - CUT]], axis=1)
        for at in (0, CUT, 2 * CUT)
    ]
    finished = in_order(gather_rows(jnp.concatenate(finished, axis=1)), xh, c)
    output, grad_tokens = finished[:, :D], finished[:, D:]

    def parcel_back(xr_, xhr):
        a, b = sum_a[36 * xr_ : 36 * xr_ + 36], sum_b[36 * xr_ : 36 * xr_ + 36]
        kv = jnp.where(xh ^ xhr == 0, b[:18, :HD], b[18:, :HD]).reshape(36, 128)
        return jnp.concatenate(
            [a[:, 256 * xhr : 256 * xhr + 256], a[:, 512:], b[:, 256 + 256 * xhr : 512 + 256 * xhr], kv],
            axis=1,
        )

    total = add(
        parcel_back(0, 0),
        fetch(parcel_back(0, 1), xh=1),
        fetch(parcel_back(1, 0), xl=1),
        fetch(parcel_back(1, 1), xl=1, xh=1),
    )
    g_kv = total[:, 640:].reshape(18, 256)
    g_kv_here = jnp.where(c == 0, g_kv[:9], g_kv[9:])
    g_kv_away = fetch(jnp.where(c == 0, g_kv[9:], g_kv[:9]).astype(bf16), c=1).astype(f32)
    g_keyval = jnp.where(
        c == 0,
        jnp.concatenate([g_kv_here, g_kv_away], axis=1),
        jnp.concatenate([g_kv_away, g_kv_here], axis=1),
    )
    g_gains = total[:, 256:264].T
    return (
        output,
        grad_tokens,
        g_gains[0],
        total[:, :256],
        g_gains[4, :8],
        g_gains[5, :8],
        g_keyval,
        total[:, 384:640].T,
        g_gains[1],
        g_gains[2],
        g_ffn[0],
        g_ffn[1],
        g_ffn[2].T,
        g_gains[3],
    )


def solution(mesh):
    row, vector, weight, weight_t = P("seq", None), P("seq"), P("seq", "mp"), P("mp", "seq")
    keyval = P(("seq", "mp"), None)
    return jax.shard_map(
        per_device,
        mesh=mesh,
        in_specs=(row, row, vector, weight, vector, vector, keyval, weight_t)
        + (vector, vector, weight, weight, weight_t, vector),
        out_specs=(row, row, vector, weight, vector, vector, keyval, weight_t)
        + (vector, vector, weight, weight, weight_t, vector),
        check_vma=False,
    )
```

```python
import jax
import jax.numpy as jnp
from jax import lax
from jax.experimental import pallas as pl
from jax.experimental.pallas import tpu as pltpu
from jax.sharding import PartitionSpec as P

D = 1152
HD = 256
WINDOW = 512
SEQ_BLOCKS = 8
ROWS = 128
KEYS = ROWS + WINDOW
EPS = 1e-06
SCALE = 0.0625
MASKED = -1e30
SIZES = {"xl": 2, "z": 4, "y": 4, "xh": 2, "c": 2}
CUT = 896

bf16 = jnp.bfloat16
f32 = jnp.float32


def coords(n):
    mp, s = n % 4, n // 4
    return {"xl": s // 16, "z": s // 4 % 4, "y": s % 4, "xh": mp // 2, "c": mp % 2}


def flat(at):
    return ((at["xl"] * 4 + at["z"]) * 4 + at["y"]) * 4 + at["xh"] * 2 + at["c"]


def fetch(x, **delta):
    pairs = []
    for n in range(128):
        at = coords(n)
        for axis, by in delta.items():
            at[axis] = (at[axis] + by) % SIZES[axis]
        pairs.append((flat(at), n))
    return lax.ppermute(x, ("seq", "mp"), pairs)


def fetch_line(x, by):
    pairs = [(n + by, n) for n in range(128) if 0 <= n + by < 128]
    return lax.ppermute(x, ("seq", "mp"), pairs)


def gather_small(x, axis):
    return [x] + [fetch(x, **{axis: k}) for k in (1, 2, 3)]


def gather_big(x, axis):
    one = fetch(x, **{axis: 1})
    three = fetch(x, **{axis: 3})
    two = [fetch(one[:2], **{axis: 1}), fetch(three[2:], **{axis: 3})]
    return [x, one, jnp.concatenate(two, axis=0), three]


def gather_onward(x, axis):
    one = fetch(x, **{axis: 1})
    return [x, one, fetch(one, **{axis: 1}), fetch(x, **{axis: 3})]


def gather_grids(a, b, first):
    line_a, line_b = lax.optimization_barrier((first(a, "z"), first(b, "y")))
    grid_a = jnp.stack(gather_big(jnp.stack(line_a), "y"), axis=1)
    grid_b = jnp.stack(gather_big(jnp.stack(line_b), "z"), axis=0)
    return grid_a.reshape(D, a.shape[-1]), grid_b.reshape(D, b.shape[-1])


def add(*terms):
    total = terms[0].astype(f32)
    for term in terms[1:]:
        total = total + term.astype(f32)
    return total


def scatter_small(blocks, axis):
    return add(blocks[0], *[fetch(blocks[k], **{axis: 4 - k}) for k in (1, 2, 3)])


def blocks_of(parts, route):
    grids = [part.reshape(4, 4, 72, part.shape[-1]) for part in parts]
    return [
        jnp.concatenate([grid[:, k] if route == 0 else grid[k] for grid in grids], axis=-1)
        for k in range(4)
    ]


def halves_out(blocks, axis):
    return fetch(blocks[2][:2], **{axis: 3}), fetch(blocks[2][2:], **{axis: 1})


def sides_of(blocks, halves):
    one = jnp.concatenate([add(blocks[1][:2], halves[0]).astype(bf16), blocks[1][2:]], axis=0)
    three = jnp.concatenate([blocks[3][:2], add(blocks[3][2:], halves[1]).astype(bf16)], axis=0)
    return one, three


def sides_out(sides, axis):
    return fetch(sides[0], **{axis: 3}), fetch(sides[1], **{axis: 1})


def gather_rows(x):
    core = fetch(x, c=1)
    far = fetch(x, xh=1)
    return jnp.concatenate([x, core, far, fetch(far, c=1)], axis=0)


def scatter_rows(x):
    got = [fetch(x[ROWS : 2 * ROWS], c=1), fetch(x[3 * ROWS :], c=1)]
    far = add(x[2 * ROWS : 3 * ROWS], got[1]).astype(bf16)
    return add(x[:ROWS], got[0], fetch(far, xh=1))


def in_order(rows, xh, c):
    grid = rows.reshape(2, 2, ROWS, rows.shape[-1])
    grid = jnp.where(xh == 0, grid, grid[::-1])
    return jnp.where(c == 0, grid, grid[:, ::-1]).reshape(rows.shape)


def dot(a, b):
    return jnp.dot(a, b, preferred_element_type=f32)


def dot_nt(a, b):
    return lax.dot_general(a, b, (((1,), (1,)), ((), ())), preferred_element_type=f32)


def dot_tn(a, b):
    return lax.dot_general(a, b, (((0,), (0,)), ((), ())), preferred_element_type=f32)


def inverse_rms(v):
    return lax.rsqrt(jnp.mean(v * v, axis=-1, keepdims=True) + EPS)


def norm_back(v, r, g, e):
    ev = e * v
    inner = jnp.mean(g * ev, axis=-1, keepdims=True)
    gain_axes = tuple(range(v.ndim - 1))
    return r * (g * e) - v * (r * r * r * inner), jnp.sum(ev * r, axis=gain_axes)


def rotary(v, cosine, sine):
    former, latter = v[..., :128], v[..., 128:]
    return jnp.concatenate([former * cosine - latter * sine, latter * cosine + former * sine], axis=-1)


def gelu_tanh(v):
    return 0.5 * v * (1.0 + jnp.tanh(0.7978845608028654 * (v + 0.044715 * v * v * v)))


def gated_hidden(gate_in, up_in):
    return gelu_tanh(gate_in) * up_in


def in_vmem(count):
    return [pl.BlockSpec(memory_space=pltpu.VMEM)] * count


def forward_kernel(hn_ref, w_ref, prior_ref, gate_ref, up_ref, sum_ref):
    hn = hn_ref[...]
    gate = dot(hn, w_ref[:, :CUT])
    up = dot(hn, w_ref[:, CUT : 2 * CUT])
    hidden = gated_hidden(gate, up).astype(bf16)
    gate_ref[...] = gate.astype(bf16)
    up_ref[...] = up.astype(bf16)
    total = dot_nt(hidden, w_ref[:, 2 * CUT :])
    if prior_ref is not None:
        total = total + prior_ref[...]
    sum_ref[...] = total.astype(sum_ref.dtype)


def ffn_forward(hn, w, prior):
    first = prior is None
    rows = hn.shape[0]
    kernel = (lambda a, b, *out: forward_kernel(a, b, None, *out)) if first else forward_kernel
    args = (hn, w) if first else (hn, w, prior)
    return pl.pallas_call(
        kernel,
        out_shape=(
            jax.ShapeDtypeStruct((rows, CUT), bf16),
            jax.ShapeDtypeStruct((rows, CUT), bf16),
            jax.ShapeDtypeStruct((rows, D), f32 if first else bf16),
        ),
        in_specs=in_vmem(len(args)),
        out_specs=tuple(in_vmem(3)),
        compiler_params=pltpu.CompilerParams(vmem_limit_bytes=36 * 2**20),
        cost_estimate=pl.CostEstimate(
            flops=6 * rows * D * CUT, bytes_accessed=12 * 2**20, transcendentals=rows * CUT
        ),
    )(*args)


def backward_kernel(d_ffn_ref, w_ref, gate_ref, up_ref, prior_ref, grads_ref, sum_ref):
    d_hidden = dot(d_ffn_ref[...], w_ref[:, 2 * CUT :])
    gate, up = gate_ref[...].astype(f32), up_ref[...].astype(f32)
    square = gate * gate
    tanh = jnp.tanh(0.7978845608028654 * (gate + 0.044715 * square * gate))
    half = 0.5 * (1.0 + tanh)
    gelu = gate * half
    slope = half + 0.5 * gate * (1.0 - tanh * tanh) * (
        0.7978845608028654 * (1.0 + 3 * 0.044715 * square)
    )
    d_gate = (d_hidden * up * slope).astype(bf16)
    d_up = (d_hidden * gelu).astype(bf16)
    grads_ref[0] = d_gate
    grads_ref[1] = d_up
    grads_ref[2] = (gelu * up).astype(bf16)
    total = dot_nt(d_gate, w_ref[:, :CUT]) + dot_nt(d_up, w_ref[:, CUT : 2 * CUT])
    if prior_ref is not None:
        total = total + prior_ref[...]
    sum_ref[...] = total.astype(sum_ref.dtype)


def ffn_backward(d_ffn, w, gate, up, prior):
    first = prior is None
    rows = d_ffn.shape[0]
    kernel = (
        (lambda a, b, g, u, *out: backward_kernel(a, b, g, u, None, *out)) if first else backward_kernel
    )
    args = (d_ffn, w, gate, up) if first else (d_ffn, w, gate, up, prior)
    return pl.pallas_call(
        kernel,
        out_shape=(
            jax.ShapeDtypeStruct((3, rows, CUT), bf16),
            jax.ShapeDtypeStruct((rows, D), f32 if first else bf16),
        ),
        in_specs=in_vmem(len(args)),
        out_specs=tuple(in_vmem(2)),
        compiler_params=pltpu.CompilerParams(vmem_limit_bytes=36 * 2**20),
        cost_estimate=pl.CostEstimate(
            flops=6 * rows * D * CUT, bytes_accessed=14 * 2**20, transcendentals=rows * CUT
        ),
    )(*args)


def weights_kernel(route, hn_ref, d_ffn_ref, grads_ref, out_ref):
    def product(left_ref):
        total = dot_tn(left_ref[...], grads_ref[0]).astype(bf16)
        for zr in range(4):
            for yr in range(4):
                block = total[72 * (4 * zr + yr) : 72 * (4 * zr + yr) + 72]
                if route == 0:
                    out_ref[yr, zr] = block
                else:
                    out_ref[zr, yr] = block

    which = pl.program_id(0)

    @pl.when(which < 2)
    def _():
        product(hn_ref)

    @pl.when(which == 2)
    def _():
        product(d_ffn_ref)


def ffn_weights(hn, d_ffn, grads, route):
    rows = hn.shape[0]
    whole = pl.BlockSpec((rows, D), lambda j: (0, 0))
    return pl.pallas_call(
        lambda *refs: weights_kernel(route, *refs),
        grid=(3,),
        out_shape=jax.ShapeDtypeStruct((4, 4, 72, 3 * CUT), bf16),
        in_specs=[whole, whole, pl.BlockSpec((1, rows, CUT), lambda j: (j, 0, 0))],
        out_specs=pl.BlockSpec((4, 4, 72, CUT), lambda j: (0, 0, 0, j)),
        compiler_params=pltpu.CompilerParams(vmem_limit_bytes=36 * 2**20),
        cost_estimate=pl.CostEstimate(
            flops=6 * rows * D * CUT, bytes_accessed=12 * 2**20, transcendentals=0
        ),
    )(hn, d_ffn, grads)


def attention_weights_kernel(xn, d_branch, gains, *refs):
    sides, outs = refs[:6], refs[6:]
    for k in range(2):
        d_q, d_kv, att = sides[3 * k : 3 * k + 3]
        out_a, out_b = outs[2 * k : 2 * k + 2]
        out_a[:, :512] = dot_tn(xn[...], d_q[...]).astype(bf16)
        out_a[:, 512:] = gains[...]
        out_b[:, :HD] = dot_tn(xn[...], d_kv[...]).astype(bf16)
        out_b[:, HD:] = dot_tn(d_branch[...], att[...]).astype(bf16)


def attention_weights(xn, d_branch, gains, here, there):
    shapes = tuple(jax.ShapeDtypeStruct((D, n), bf16) for n in (640, 768, 640, 768))
    return pl.pallas_call(
        attention_weights_kernel,
        out_shape=shapes,
        in_specs=in_vmem(9),
        out_specs=tuple(in_vmem(4)),
        compiler_params=pltpu.CompilerParams(vmem_limit_bytes=24 * 2**20),
        cost_estimate=pl.CostEstimate(
            flops=2 * ROWS * D * 2560, bytes_accessed=8 * 2**20, transcendentals=0
        ),
    )(xn, d_branch, gains, *here, *there)


def per_device(
    tokens,
    grad_out,
    attn_pre_gain,
    w_query,
    query_gain,
    key_gain,
    w_keyval,
    w_out,
    attn_post_gain,
    ffn_pre_gain,
    w_gate,
    w_up,
    w_down,
    ffn_post_gain,
):
    seq = lax.axis_index("seq")
    mp = lax.axis_index("mp")
    xl, z, y = seq // 16, seq // 4 % 4, seq % 4
    xh, c = mp // 2, mp % 2

    kv_mine = lax.dynamic_slice_in_dim(w_keyval, 256 * c, 256, 1)
    kv_other = fetch(lax.dynamic_slice_in_dim(w_keyval, 256 * (1 - c), 256, 1), c=1)
    kv18 = jnp.where(
        c == 0,
        jnp.concatenate([kv_mine, kv_other], axis=0),
        jnp.concatenate([kv_other, kv_mine], axis=0),
    )
    short = jnp.pad(jnp.stack([query_gain, key_gain], axis=1), ((0, 28), (0, 0)))
    gains = jnp.stack([attn_pre_gain, attn_post_gain, ffn_pre_gain, ffn_post_gain], axis=1)
    gains = jnp.pad(jnp.concatenate([gains, short], axis=1), ((0, 0), (0, 122)))
    parcel = jnp.concatenate([w_query, gains, w_out.T, kv18.reshape(36, 128)], axis=1)
    half = fetch_line(lax.dynamic_slice_in_dim(tokens, 256 * c, 256, 0), -4)
    parcels = [
        [parcel, fetch(parcel, xh=1)],
        [fetch(parcel, xl=1), fetch(parcel, xl=1, xh=1)],
    ]
    parcels, half = lax.optimization_barrier((parcels, half))

    def kv36(pair):
        own, far = pair[0][:, 640:].reshape(18, 256), pair[1][:, 640:].reshape(18, 256)
        return jnp.where(
            xh == 0, jnp.concatenate([own, far], axis=0), jnp.concatenate([far, own], axis=0)
        )

    block_a = jnp.concatenate(
        [jnp.concatenate([p[0][:, :256], p[1][:, :256], p[0][:, 256:384]], axis=1) for p in parcels],
        axis=0,
    )
    block_b = jnp.concatenate(
        [jnp.concatenate([kv36(p), p[0][:, 384:640], p[1][:, 384:640]], axis=1) for p in parcels],
        axis=0,
    )
    part_a, part_b = gather_grids(block_a, block_b, gather_onward)
    part_ao = fetch(part_a[:, :512], c=1)
    part_bo = fetch(part_b, c=1)

    units = w_down.shape[0]
    ffn_own = jnp.stack([w_gate, w_up, w_down.T])
    ffn_own = jnp.pad(ffn_own, ((0, 0), (0, 0), (0, 2 * CUT - units)))
    ffn_own = jnp.stack(
        [
            jnp.concatenate([ffn_own[k, :, half * CUT : half * CUT + CUT] for k in range(3)], axis=1)
            for half in range(2)
        ]
    )
    ffn_own, block_a = lax.optimization_barrier((ffn_own, block_a))
    ffn_pair = jnp.concatenate([ffn_own, fetch(ffn_own, xl=1)], axis=1)
    ffn_pair, part_a, part_b = lax.optimization_barrier((ffn_pair, part_a, part_b))
    part_fa, part_fb = gather_grids(ffn_pair[0], ffn_pair[1], gather_onward)

    half_other = fetch(half, c=1)
    before = jnp.where(
        c == 0,
        jnp.concatenate([half, half_other], axis=0),
        jnp.concatenate([half_other, half], axis=0),
    )
    rows = lax.dynamic_slice_in_dim(jnp.concatenate([before, tokens], axis=0), ROWS * mp, KEYS, 0)
    column = jnp.arange(D, dtype=jnp.int32)
    zr, yr, xr, place = column // 288, column // 72 % 4, column // 36 % 2, column % 36
    owner = (xl ^ xr) * 16 + (z + zr) % 4 * 4 + (y + yr) % 4
    order = (column[:, None] == (owner * 36 + place)[None, :]).astype(bf16)
    short_owner = jnp.where(place < 8, owner * 8 + place, -1)
    short_order = (short_owner[:, None] == jnp.arange(HD, dtype=jnp.int32)[None, :]).astype(bf16)
    x_keys = dot(rows, order).astype(bf16).astype(f32)
    x = x_keys[WINDOW:]
    e_out = dot(lax.dynamic_slice_in_dim(grad_out, ROWS * mp, ROWS, 0), order).astype(bf16).astype(f32)
    r_keys = inverse_rms(x_keys)

    gain_cols = part_a[:, 512:]
    gain_rows = gain_cols[:, :8].T.astype(f32)
    pre_gain, post_gain, ffn_pre, ffn_post = (gain_rows[k : k + 1] for k in range(4))
    short_rows = dot_tn(gain_cols, short_order)
    qnorm_gain, knorm_gain = short_rows[4:5], short_rows[5:6]

    first_pos = seq % SEQ_BLOCKS * 512 + ROWS * mp
    positions = (first_pos - WINDOW + jnp.arange(KEYS, dtype=jnp.int32)).astype(f32)
    exponent = jnp.arange(HD // 2, dtype=f32) * (-2.0 / HD)
    angle = positions[:, None] * jnp.power(10000.0, exponent)[None, :]
    cosine, sine = jnp.cos(angle), jnp.sin(angle)
    cos_q, sin_q = cosine[WINDOW:], sine[WINDOW:]
    xn_keys = (x_keys * r_keys * pre_gain).astype(bf16)
    xn = xn_keys[WINDOW:]
    q_raw = [dot(xn, part_a[:, :512]), dot(xn, part_ao)]
    q_raw = jnp.stack([q_raw[h // 2][:, h % 2 * HD : h % 2 * HD + HD] for h in range(4)])
    kv_here, kv_there = dot(xn_keys, part_b[:, :HD]), dot(xn_keys, part_bo[:, :HD])
    key_raw = jnp.where(c == 0, kv_here, kv_there)
    values = jnp.where(c == 0, kv_there, kv_here).astype(bf16)
    r_q, r_k = inverse_rms(q_raw), inverse_rms(key_raw)
    query = rotary(q_raw * r_q * qnorm_gain, cos_q, sin_q).astype(bf16).reshape(4 * ROWS, HD)
    keys = rotary(key_raw * r_k * knorm_gain, cosine, sine).astype(bf16)
    row_ids = jnp.arange(ROWS, dtype=jnp.int32)[:, None]
    key_ids = jnp.arange(KEYS, dtype=jnp.int32)[None, :]
    allowed = (key_ids > row_ids) & (key_ids <= row_ids + WINDOW) & (key_ids + first_pos >= WINDOW)
    score = dot_nt(query, keys).reshape(4, ROWS, KEYS) * SCALE
    score = jnp.where(allowed[None], score, MASKED)
    peak = jnp.max(score, axis=-1, keepdims=True)
    weight = jnp.exp(score - peak)
    prob = weight / jnp.sum(weight, axis=-1, keepdims=True)
    prob_low = prob.astype(bf16).reshape(4 * ROWS, KEYS)
    att = dot(prob_low, values).astype(bf16).reshape(4, ROWS, HD)
    att = jnp.concatenate([att[h] for h in range(4)], axis=1)
    out_own, out_other = part_b[:, HD:], part_bo[:, HD:]
    branch = dot_nt(att[:, :512], out_own) + dot_nt(att[:, 512:], out_other)
    r_branch = inverse_rms(branch)
    mid = x + branch * r_branch * post_gain
    r_mid = inverse_rms(mid)
    hn_rows = (mid * r_mid * ffn_pre).astype(bf16)

    hn = gather_rows(hn_rows)
    gate_a, up_a, partial = ffn_forward(hn, part_fa, None)
    gate_b, up_b, partial = ffn_forward(hn, part_fb, partial)
    ffn = scatter_rows(partial)
    r_ffn = inverse_rms(ffn)
    output_rows = (mid + ffn * r_ffn * ffn_post).astype(bf16)
    d_ffn_rows, grad_ffn_post = norm_back(ffn, r_ffn, ffn_post, e_out)
    d_ffn = gather_rows(d_ffn_rows.astype(bf16))
    grads_a, partial = ffn_backward(d_ffn, part_fa, gate_a, up_a, None)
    grads_b, partial = ffn_backward(d_ffn, part_fb, gate_b, up_b, partial)
    d_hn = scatter_rows(partial)
    g_a, g_b = ffn_weights(hn, d_ffn, grads_a, 0), ffn_weights(hn, d_ffn, grads_b, 1)
    halves = halves_out(g_a, "y"), halves_out(g_b, "z")

    d_mid, grad_ffn_pre = norm_back(mid, r_mid, ffn_pre, d_hn)
    d_mid = d_mid + e_out
    d_branch, grad_post = norm_back(branch, r_branch, post_gain, d_mid)
    d_branch = d_branch.astype(bf16)
    d_att = [dot(d_branch, out_own), dot(d_branch, out_other)]
    d_att = jnp.stack([d_att[h // 2][:, h % 2 * HD : h % 2 * HD + HD] for h in range(4)])
    d_att = d_att.astype(bf16).reshape(4 * ROWS, HD)
    d_att, halves, output_rows = lax.optimization_barrier((d_att, halves, output_rows))
    ffn_sides = sides_of(g_a, halves[0]), sides_of(g_b, halves[1])
    d_prob = dot_nt(d_att, values).reshape(4, ROWS, KEYS)
    delta = jnp.sum(prob * d_prob, axis=-1, keepdims=True)
    d_score = (prob * (d_prob - delta)).astype(bf16).reshape(4 * ROWS, KEYS)
    d_query = dot(d_score, keys).reshape(4, ROWS, HD) * SCALE
    d_kv = jnp.concatenate(
        [dot_tn(d_score, query) * SCALE, dot_tn(prob_low, d_att)], axis=1
    ).reshape(5, ROWS, 2 * HD)
    d_kv_low = d_kv[:4].astype(bf16)
    d_q_raw, grad_query_gain = norm_back(q_raw, r_q, qnorm_gain, rotary(d_query, cos_q, -sin_q))
    d_q_raw = d_q_raw.astype(bf16)
    d_q_own = jnp.concatenate([d_q_raw[0], d_q_raw[1]], axis=1)
    d_q_other = jnp.concatenate([d_q_raw[2], d_q_raw[3]], axis=1)
    d_kv_low, ffn_sides = lax.optimization_barrier((d_kv_low, ffn_sides))
    d_kv_away = [fetch_line(d_kv_low[k], 4 - k) for k in range(4)]
    ffn_sides = sides_out(ffn_sides[0], "y"), sides_out(ffn_sides[1], "z")
    d_kv = add(d_kv[4], *d_kv_away)
    d_key = rotary(d_kv[:, :HD], cos_q, -sin_q)
    d_key_raw, grad_key_gain = norm_back(key_raw[WINDOW:], r_k[WINDOW:], knorm_gain, d_key)
    d_key_raw = d_key_raw.astype(bf16)
    d_value = d_kv[:, HD:].astype(bf16)
    d_here = jnp.where(c == 0, d_key_raw, d_value)
    d_there = jnp.where(c == 0, d_value, d_key_raw)
    d_xn = (
        dot_nt(d_q_own, part_a[:, :512])
        + dot_nt(d_q_other, part_ao)
        + dot_nt(d_here, part_b[:, :HD])
        + dot_nt(d_there, part_bo[:, :HD])
    )
    d_x, grad_pre = norm_back(x, r_keys[WINDOW:], pre_gain, d_xn)
    d_tokens = (d_mid + d_x).astype(bf16)

    short_grads = dot_nt(jnp.stack([grad_query_gain, grad_key_gain]).astype(bf16), short_order)
    gain_grads = jnp.concatenate(
        [jnp.stack([grad_pre, grad_post, grad_ffn_pre, grad_ffn_post]), short_grads]
    )
    gain_grads = jnp.pad(gain_grads, ((0, 2), (0, 0))).T.astype(bf16)
    gain_grads = jnp.pad(gain_grads, ((0, 0), (0, 120)))
    own_a, own_b, other_a, other_b = attention_weights(
        xn,
        d_branch,
        gain_grads,
        (d_q_own, d_here, att[:, :512]),
        (d_q_other, d_there, att[:, 512:]),
    )
    finished = [dot_nt(v, order).astype(bf16) for v in (output_rows, d_tokens)]
    own_a, own_b, other_a, other_b, ffn_sides, finished = lax.optimization_barrier(
        (own_a, own_b, other_a, other_b, ffn_sides, finished)
    )
    sum_a = add(own_a, fetch(other_a, c=1)).astype(bf16)
    sum_b = add(own_b, fetch(other_b, c=1)).astype(bf16)
    sum_a, sum_b, ffn_sides = lax.optimization_barrier((sum_a, sum_b, ffn_sides))
    line_a, line_b = add(g_a[0], *ffn_sides[0]).astype(bf16), add(g_b[0], *ffn_sides[1]).astype(bf16)
    g_ffn = jnp.stack(
        [
            scatter_small([line_a[k] for k in range(4)], "z"),
            scatter_small([line_b[k] for k in range(4)], "y"),
        ]
    )
    sum_a, sum_b = blocks_of([sum_a], 0), blocks_of([sum_b], 1)
    halves = halves_out(sum_a, "y"), halves_out(sum_b, "z")
    halves, finished = lax.optimization_barrier((halves, finished))
    sides = sides_of(sum_a, halves[0]), sides_of(sum_b, halves[1])
    sides = sides_out(sides[0], "y"), sides_out(sides[1], "z")
    sides = lax.optimization_barrier(sides)
    line_a, line_b = add(sum_a[0], *sides[0]).astype(bf16), add(sum_b[0], *sides[1]).astype(bf16)
    sum_a = scatter_small([line_a[k] for k in range(4)], "z").astype(bf16)
    sum_b = scatter_small([line_b[k] for k in range(4)], "y").astype(bf16)

    g_ffn = add(g_ffn[:, :36], fetch(g_ffn[:, 36:].astype(bf16), xl=1))
    g_ffn = [
        jnp.concatenate([g_ffn[0, :, at : at + CUT], g_ffn[1, :, at : at + units - CUT]], axis=1)
        for at in (0, CUT, 2 * CUT)
    ]
    finished = in_order(gather_rows(jnp.concatenate(finished, axis=1)), xh, c)
    output, grad_tokens = finished[:, :D], finished[:, D:]

    def parcel_back(xr_, xhr):
        a, b = sum_a[36 * xr_ : 36 * xr_ + 36], sum_b[36 * xr_ : 36 * xr_ + 36]
        kv = jnp.where(xh ^ xhr == 0, b[:18, :HD], b[18:, :HD]).reshape(36, 128)
        return jnp.concatenate(
            [a[:, 256 * xhr : 256 * xhr + 256], a[:, 512:], b[:, 256 + 256 * xhr : 512 + 256 * xhr], kv],
            axis=1,
        )

    total = add(
        parcel_back(0, 0),
        fetch(parcel_back(0, 1), xh=1),
        fetch(parcel_back(1, 0), xl=1),
        fetch(parcel_back(1, 1), xl=1, xh=1),
    )
    g_kv = total[:, 640:].reshape(18, 256)
    g_kv_here = jnp.where(c == 0, g_kv[:9], g_kv[9:])
    g_kv_away = fetch(jnp.where(c == 0, g_kv[9:], g_kv[:9]).astype(bf16), c=1).astype(f32)
    g_keyval = jnp.where(
        c == 0,
        jnp.concatenate([g_kv_here, g_kv_away], axis=1),
        jnp.concatenate([g_kv_away, g_kv_here], axis=1),
    )
    g_gains = total[:, 256:264].T
    return (
        output,
        grad_tokens,
        g_gains[0],
        total[:, :256],
        g_gains[4, :8],
        g_gains[5, :8],
        g_keyval,
        total[:, 384:640].T,
        g_gains[1],
        g_gains[2],
        g_ffn[0],
        g_ffn[1],
        g_ffn[2].T,
        g_gains[3],
    )


def solution(mesh):
    row, vector, weight, weight_t = P("seq", None), P("seq"), P("seq", "mp"), P("mp", "seq")
    keyval = P(("seq", "mp"), None)
    return jax.shard_map(
        per_device,
        mesh=mesh,
        in_specs=(row, row, vector, weight, vector, vector, keyval, weight_t)
        + (vector, vector, weight, weight, weight_t, vector),
        out_specs=(row, row, vector, weight, vector, vector, keyval, weight_t)
        + (vector, vector, weight, weight, weight_t, vector),
        check_vma=False,
    )
```
